128 devices in a mesh: gx: 16 (over y, x_hi, core), gy: 8 (over x_lo, z).
Axes of the slice: x: 4 (x_hi: 2, x_lo: 2; x = x_hi * 2 + x_lo), y: 4, z: 4, core: 2. Of those that a mesh axis runs over, the one named last changes fastest.
Arguments:
- tracer: float32 [2, 16, 3584, 2048], P(None, None, 'gx', 'gy'), may hold values from -6 to 6
- zonal_flow: bfloat16 [16, 3584, 2048], P(None, 'gx', 'gy'), may hold values from -3 to 3
- meridional_flow: bfloat16 [16, 3584, 2048], P(None, 'gx', 'gy'), may hold values from -3 to 3
- surface_prev: float32 [3584, 2048], P('gx', 'gy'), may hold values from -6 to 6
- transport_x: float32 [3584, 2048], P('gx', 'gy'), may hold values from -6 to 6
- transport_y: float32 [3584, 2048], P('gx', 'gy'), may hold values from -6 to 6
- land_mask: int32 [3584, 2048], P('gx', 'gy'), may hold values 0 or 1
- levels: int32 [3584, 2048], P('gx', 'gy'), may hold values from 1 to 16
Outputs:
- tracer_next: float32 [2, 16, 3584, 2048], P(None, None, 'gx', 'gy')
- surface: float32 [3584, 2048], P('gx', 'gy')
- transport_x_next: float32 [3584, 2048], P('gx', 'gy')
- transport_y_next: float32 [3584, 2048], P('gx', 'gy')
The draws below stay inside these ranges and needn't reach their ends.
All inputs are finite; a program needn't handle non-finite values. No bound on the sum of `land_mask` on one device may be relied on, other than what follows from the above.
Results may differ from the reference program's by a relative error of at most 0.0003.
Values sent between devices are 32-bit elements; how exact they have to be, the bound alone decides.
A program may use at most 192 MiB of HBM per device.

```python
import jax
import jax.numpy as jnp
from jax import lax

LEVELS = 16
ITERS = 4
NX = 3584
NY = 2048


def plant(entries, rng, low, largest):
    longest = entries.shape.index(max(entries.shape))
    spots = []
    for shift in (0, 1):
        where = [jax.random.randint(jax.random.fold_in(rng, axis), (), 0, length) for axis, length in enumerate(entries.shape)]
        where[longest] = (where[longest] + shift) % entries.shape[longest]
        spots.append(tuple(where))
    return entries.at[spots[0]].set(low).at[spots[1]].set(largest)


def steps_of(stream_key, shape, cuts, smallest, largest):
    gain, own = 1.0, jax.random.fold_in(stream_key, 6)
    for position, blocks in cuts:
        heights = jnp.exp(jax.random.uniform(jax.random.fold_in(own, position), (blocks,), jnp.float32, smallest / len(cuts), largest / len(cuts)))
        gain = gain * jnp.repeat(heights, shape[position] // blocks).reshape([-1 if axis == position else 1 for axis in range(len(shape))])
    return gain


def gaussian(rng, dims, scale, most, cuts=(), kind=jnp.bfloat16):
    values = jax.random.normal(rng, dims, jnp.float32) * scale
    if len(cuts) > 0:
        values = steps_of(rng, dims, cuts, -0.22, 0.18) * values
    return jnp.clip(values, min=-most, max=most).astype(kind)


def setup_inputs(seed: int = 0) -> dict:
    splits = jax.random.split(jax.random.key(seed), 9)
    tracer = gaussian(splits[0], (2, LEVELS, NX, NY), 1.0, 6.0, ((2, 16), (3, 8)), jnp.float32)
    zonal_flow = gaussian(splits[1], (LEVELS, NX, NY), 0.5, 3.0, ((1, 16), (2, 8)))
    meridional_flow = gaussian(splits[2], (LEVELS, NX, NY), 0.5, 3.0, ((1, 16), (2, 8)))
    surface_prev = gaussian(splits[3], (NX, NY), 1.0, 6.0, ((0, 16), (1, 8)), jnp.float32)
    transport_x = gaussian(splits[4], (NX, NY), 1.0, 6.0, ((0, 16), (1, 8)), jnp.float32)
    transport_y = gaussian(splits[5], (NX, NY), 1.0, 6.0, ((0, 16), (1, 8)), jnp.float32)
    land_mask = plant((jax.random.randint(splits[6], (NX, NY), 0, 4) < 3).astype(jnp.int32), jax.random.fold_in(splits[6], 1), 0, 1)
    levels = plant(jax.random.randint(splits[7], (NX, NY), 1, LEVELS + 1), jax.random.fold_in(splits[7], 1), 1, LEVELS).astype(jnp.int32)
    return {"tracer": tracer, "zonal_flow": zonal_flow, "meridional_flow": meridional_flow, "surface_prev": surface_prev, "transport_x": transport_x, "transport_y": transport_y, "land_mask": land_mask, "levels": levels}


OFFSETS = ((1, 0, 1.0), (-1, 0, 1.0), (0, 1, 1.0), (0, -1, 1.0), (1, 1, 0.5), (1, -1, 0.5), (-1, 1, 0.5), (-1, -1, 0.5))


def cycle_pad(field):
    wide = jnp.concatenate([field[..., -1:, :], field, field[..., :1, :]], -2)
    zero = jnp.zeros_like(wide[..., :1])
    return jnp.concatenate([zero, wide, zero], -1)


def advance(wide, zonal, merid):
    centre = wide[..., 1:-1, 1:-1]
    east = wide[..., 2:, 1:-1]
    west = wide[..., :-2, 1:-1]
    north = wide[..., 1:-1, 2:]
    south = wide[..., 1:-1, :-2]
    values = centre[:2]
    wet_here = centre[2]
    lap = east[2] * (east[:2] - values) + west[2] * (west[:2] - values)
    lap = lap + north[2] * (north[:2] - values) + south[2] * (south[:2] - values)
    speed_x = zonal.astype(jnp.float32)
    speed_y = merid.astype(jnp.float32)
    adv = speed_x * (east[2] * east[:2] - west[2] * west[:2]) * 0.5
    adv = adv + speed_y * (north[2] * north[:2] - south[2] * south[:2]) * 0.5
    return values + wet_here * (0.2 * lap - 0.5 * adv)


def couplings(depth_pad):
    depth = depth_pad[1:-1, 1:-1]
    count_x, count_y = depth.shape
    ocean = (depth > 0).astype(jnp.float32)
    weights = []
    for shift_x, shift_y, factor in OFFSETS:
        other = depth_pad[1 + shift_x:1 + shift_x + count_x, 1 + shift_y:1 + shift_y + count_y]
        weights.append(4.0 * factor * ocean * (other > 0).astype(jnp.float32) * 0.5 * (depth + other))
    diag = 0.5 + sum(weights)
    return weights, diag


def operate(weights, diag, surf_pad):
    count_x, count_y = diag.shape
    total = diag * surf_pad[1:-1, 1:-1]
    for (shift_x, shift_y, factor), weight in zip(OFFSETS, weights):
        total = total - weight * surf_pad[1 + shift_x:1 + shift_x + count_x, 1 + shift_y:1 + shift_y + count_y]
    return total


def reference(tracer, zonal_flow, meridional_flow, surface_prev, transport_x, transport_y, land_mask, levels):
    ocean_col = land_mask == 1

    def level_step(items):
        temp, zonal, merid, level = items
        wet_k = (ocean_col & (level < levels)).astype(jnp.float32)
        wide = cycle_pad(jnp.concatenate([temp, wet_k[None]], 0))
        return advance(wide, zonal, merid)

    level_ids = jnp.arange(LEVELS, dtype=jnp.int32)
    stepped = lax.map(level_step, (jnp.moveaxis(tracer, 1, 0), zonal_flow, meridional_flow, level_ids))
    tracer_next = jnp.moveaxis(stepped, 0, 1)

    def column(carry, items):
        press, accum = carry
        temp, level = items
        wet_k = (ocean_col & (level < levels)).astype(jnp.float32)
        press = press + wet_k * (0.8 * temp[0] - 0.6 * temp[1])
        accum = accum + wet_k * press
        return (press, accum), None

    zero = jnp.zeros(surface_prev.shape, jnp.float32)
    (press, accum), _ = lax.scan(column, (zero, zero), (jnp.moveaxis(tracer, 1, 0), level_ids))
    force = accum / LEVELS
    depth = (levels * land_mask).astype(jnp.float32) / LEVELS
    ocean = (depth > 0).astype(jnp.float32)
    padded = cycle_pad(jnp.stack([depth, transport_x, transport_y]))
    weights, diag = couplings(padded[0])
    ocean_pad = (padded[0] > 0).astype(jnp.float32)
    flux_x = ocean_pad * padded[1]
    flux_y = ocean_pad * padded[2]
    div = (flux_x[2:, 1:-1] - flux_x[:-2, 1:-1]) * 0.5 + (flux_y[1:-1, 2:] - flux_y[1:-1, :-2]) * 0.5
    rhs = 0.5 * surface_prev + force - 0.5 * div
    peak = jnp.max(diag)
    lowest = 0.5 / peak
    scale = 1.0 / (1.0 - lowest)
    surf = surface_prev
    resid = rhs - operate(weights, diag, cycle_pad(surf))
    delta = resid / diag
    omega = 2.0
    surf = surf + delta
    for step in range(1, ITERS):
        resid = rhs - operate(weights, diag, cycle_pad(surf))
        omega = 1.0 / (1.0 - omega / (4.0 * scale * scale))
        delta = omega * resid / diag + (omega - 1.0) * delta
        surf = surf + delta
    surf_pad = cycle_pad(surf)
    next_x = ocean * (transport_x - 0.5 * (surf_pad[2:, 1:-1] - surf_pad[:-2, 1:-1]) * 0.5)
    next_y = ocean * (transport_y - 0.5 * (surf_pad[1:-1, 2:] - surf_pad[1:-1, :-2]) * 0.5)
    return tracer_next, surf, next_x, next_y
```

```python
import jax
import jax.numpy as jnp
from jax import lax
from jax.experimental import pallas as pl
from jax.experimental.pallas import tpu as pltpu
from jax.sharding import PartitionSpec as P

MESH = pl.DeviceIdType.MESH
F32 = jnp.float32
I32 = jnp.int32

LEVELS = 16
ROWS = 224
COLS = 256
LANES = 128
HALO = 8
FIRST = 16
LAST = FIRST + ROWS
EXT = 256
GROUP = 32
NGROUPS = ROWS // GROUP
CHUNK = 16


def lane_ids(rows):
    return lax.broadcasted_iota(I32, (rows, LANES), 1)


def to_north(tiles, lanes):
    moved = [pltpu.roll(t, LANES - 1, 1) for t in tiles]
    n = len(tiles)
    return [jnp.where(lanes == LANES - 1, moved[(i + 1) % n], moved[i]) for i in range(n)]


def to_south(tiles, lanes):
    moved = [pltpu.roll(t, 1, 1) for t in tiles]
    n = len(tiles)
    return [jnp.where(lanes == 0, moved[(i - 1) % n], moved[i]) for i in range(n)]


def nine_sum(ref, r0, rows, lanes):
    sides, inner = [], []
    for t in range(3):
        here = ref[t, pl.ds(r0, rows), :]
        pair = ref[t, pl.ds(r0 + 1, rows), :] + ref[t, pl.ds(r0 - 1, rows), :]
        sides.append(pair)
        inner.append(here + 0.5 * pair)
    north = to_north(inner, lanes)
    south = to_south(inner, lanes)
    return [sides[t] + (north[t] + south[t]) for t in range(3)]


def step_kernel(
    tr_hbm, u_hbm, v_hbm, e0_hbm, tx_hbm, ty_hbm, mask_hbm, lev_hbm,
    out_ref, ext_ref, own_ref, peak_ref,
    trs, us, vs, mask_s, lev_s, raw_s,
    lx, fx, mx, a1, a2, inv, xa, ya, xb, yb, zx, cnt,
    psc, row_e, row_w, got_e, got_w, pack_n, pack_s, got_n, got_s,
    l_n, l_s, l_th, l_co, f_n, f_s, f_th, f_co,
    mine, mid, max_x, max_y,
    in_sem, tr_sem, uv_sem, send_sem, recv_sem,
):
    gx = lax.axis_index("gx")
    gy = lax.axis_index("gy")
    nx = lax.axis_size("gx")
    ny = lax.axis_size("gy")
    east, west = lax.rem(gx + 1, nx), lax.rem(gx + nx - 1, nx)
    north, south = lax.rem(gy + 1, ny), lax.rem(gy + ny - 1, ny)
    corners = ((east, north), (east, south), (west, north), (west, south))

    barrier = pltpu.get_barrier_semaphore()
    for d in range(1, nx):
        pl.semaphore_signal(barrier, inc=1, device_id=(lax.rem(gx + d, nx), gy), device_id_type=MESH)
    for d in range(1, ny):
        pl.semaphore_signal(barrier, inc=1, device_id=(gx, lax.rem(gy + d, ny)), device_id_type=MESH)
    for c in corners:
        pl.semaphore_signal(barrier, inc=1, device_id=c, device_id_type=MESH)

    def flat_copy(src, dst, slot):
        copies = []
        for t in range(2):
            copies.append(
                pltpu.make_async_copy(
                    src.at[:, pl.ds(t * LANES, LANES)], dst(t), in_sem.at[2 * slot + t]
                )
            )
        for c in copies:
            c.start()
        return copies

    c_mask = flat_copy(mask_hbm, lambda t: mask_s.at[t], 0)
    c_lev = flat_copy(lev_hbm, lambda t: lev_s.at[t], 1)
    c_tx = flat_copy(tx_hbm, lambda t: raw_s.at[0, t], 2)
    c_ty = flat_copy(ty_hbm, lambda t: raw_s.at[1, t], 3)
    c_e0 = flat_copy(e0_hbm, lambda t: fx.at[0, t, pl.ds(FIRST, ROWS), :], 4)

    def group_copy(g):
        rows = pl.ds(pl.multiple_of(g * GROUP, GROUP), GROUP)
        return pltpu.make_async_copy(
            tr_hbm.at[:, :, rows, :], trs.at[:, :, rows, :], tr_sem.at[g]
        )

    for g in range(NGROUPS):
        group_copy(g).start()
    c_u = pltpu.make_async_copy(u_hbm, us, uv_sem.at[0])
    c_v = pltpu.make_async_copy(v_hbm, vs, uv_sem.at[1])
    c_u.start()
    c_v.start()

    for ref in (mx, lx, xa, ya, xb, yb):
        for t in range(3):
            ref[t, pl.ds(0, HALO), :] = jnp.zeros((HALO, LANES), F32)
            ref[t, pl.ds(EXT - HALO, HALO), :] = jnp.zeros((HALO, LANES), F32)

    for c in c_mask + c_lev:
        c.wait()
    for t in range(2):
        depth = (lev_s[t] * mask_s[t]).astype(F32)
        lx[t, pl.ds(FIRST, ROWS), :] = depth
        turned = jnp.transpose(depth)
        if t == 0:
            l_s[...] = turned[:HALO]
        else:
            l_n[...] = turned[LANES - HALO :]
    for c in c_tx + c_ty + c_e0:
        c.wait()
    for t in range(2):
        wet = lx[t, pl.ds(FIRST, ROWS), :] > 0.0
        own_ref[2, t] = jnp.where(wet, 1.0, 0.0)
        for i in range(2):
            value = jnp.where(wet, raw_s[i, t], 0.0)
            own_ref[i, t] = value
            fx[2 + i, t, pl.ds(FIRST, ROWS), :] = value

    glanes = lane_ids(GROUP)

    def force_group(g, carry):
        group_copy(g).wait()
        r0 = pl.multiple_of(g * GROUP, GROUP)
        depth = [lx[t, pl.ds(r0 + FIRST, GROUP), :] for t in range(2)]
        total = [jnp.zeros((GROUP, LANES), F32) for _ in range(2)]
        col_n = jnp.zeros((GROUP, LANES), F32)
        col_s = jnp.zeros((GROUP, LANES), F32)
        for k in range(LEVELS):
            for t in range(2):
                lanes = pl.ds(t * LANES, LANES)
                left = depth[t] - float(k)
                wet = left > 0.0
                t0 = trs[0, k, pl.ds(r0, GROUP), lanes]
                t1 = trs[1, k, pl.ds(r0, GROUP), lanes]
                total[t] = total[t] + jnp.maximum(left, 0.0) * (0.8 * t0 - 0.6 * t1)
                for i, value in enumerate((t0, t1)):
                    plane = i * LEVELS + k
                    value = jnp.where(wet, value, 0.0)
                    psc[plane, t, pl.ds(r0 + HALO, GROUP), :] = value
                    if t == 0:
                        moved = value if plane == 0 else pltpu.roll(value, plane, 1)
                        col_s = jnp.where(glanes == plane, moved, col_s)
                    else:
                        moved = pltpu.roll(value, plane + 1, 1)
                        col_n = jnp.where(glanes == plane, moved, col_n)
        pack_n[pl.ds(r0, GROUP), :] = col_n
        pack_s[pl.ds(r0, GROUP), :] = col_s
        for t in range(2):
            rows = pl.ds(r0 + FIRST, GROUP)
            fx[1, t, rows, :] = total[t] * (1.0 / LEVELS) + 0.5 * fx[0, t, rows, :]
        return carry

    lax.fori_loop(0, NGROUPS, force_group, 0)

    for plane in range(2 * LEVELS):
        for t in range(2):
            row_w[pl.ds(2 * plane + t, 1), :] = psc[plane, t, pl.ds(HALO, 1), :]
            row_e[pl.ds(2 * plane + t, 1), :] = psc[plane, t, pl.ds(HALO + ROWS - 1, 1), :]
    for f in range(4):
        f_s[f] = jnp.transpose(fx[f, 0, pl.ds(FIRST, ROWS), :])[:HALO]
        f_n[f] = jnp.transpose(fx[f, 1, pl.ds(FIRST, ROWS), :])[LANES - HALO :]

    pl.semaphore_wait(barrier, (nx - 1) + (ny - 1) + 4)

    started = [0]

    def remote(src, dst, who):
        slot = started[0]
        started[0] += 1
        copy = pltpu.make_async_remote_copy(
            src_ref=src,
            dst_ref=dst,
            send_sem=send_sem.at[slot],
            recv_sem=recv_sem.at[slot],
            device_id=who,
            device_id_type=MESH,
        )
        copy.start()
        return copy

    high, low = pl.ds(LAST - HALO, HALO), pl.ds(FIRST, HALO)
    below, above = pl.ds(FIRST - HALO, HALO), pl.ds(LAST, HALO)
    both = pl.ds(0, 2)
    depth_copies = [
        remote(l_co_src, l_co.at[i], who)
        for i, (l_co_src, who) in enumerate(
            (
                (lx.at[1, high, :], (east, north)),
                (lx.at[0, high, :], (east, south)),
                (lx.at[1, low, :], (west, north)),
                (lx.at[0, low, :], (west, south)),
            )
        )
    ]
    depth_copies += [
        remote(lx.at[both, high, :], lx.at[both, below, :], (east, gy)),
        remote(lx.at[both, low, :], lx.at[both, above, :], (west, gy)),
        remote(l_n, l_th.at[pl.ds(LANES - HALO, HALO), :], (gx, north)),
        remote(l_s, l_th.at[pl.ds(0, HALO), :], (gx, south)),
    ]
    every = pl.ds(0, 4)
    field_copies = [
        remote(fx.at[every, both, high, :], fx.at[every, both, below, :], (east, gy)),
        remote(fx.at[every, both, low, :], fx.at[every, both, above, :], (west, gy)),
        remote(f_n, f_th.at[:, pl.ds(LANES - HALO, HALO), :], (gx, north)),
        remote(f_s, f_th.at[:, pl.ds(0, HALO), :], (gx, south)),
        remote(fx.at[every, 1, high, :], f_co.at[0], (east, north)),
        remote(fx.at[every, 0, high, :], f_co.at[1], (east, south)),
        remote(fx.at[every, 1, low, :], f_co.at[2], (west, north)),
        remote(fx.at[every, 0, low, :], f_co.at[3], (west, south)),
    ]
    tracer_copies = [
        remote(row_e, got_w, (east, gy)),
        remote(row_w, got_e, (west, gy)),
        remote(pack_n, got_s, (gx, north)),
        remote(pack_s, got_n, (gx, south)),
    ]

    lanes8 = lane_ids(HALO)
    lanes_all = lane_ids(ROWS)

    def inside(lanes):
        return ((lanes < HALO) & (gy < ny - 1)) | ((lanes >= LANES - HALO) & (gy > 0))

    def third_tile(dst, turned, co):
        keep8 = inside(lanes8)
        dst[2, pl.ds(FIRST, ROWS), :] = jnp.where(inside(lanes_all), jnp.transpose(turned), 0.0)
        dst[2, below, :] = jnp.where(keep8, jnp.where(lanes8 < HALO, co[1], co[0]), 0.0)
        dst[2, above, :] = jnp.where(keep8, jnp.where(lanes8 < HALO, co[3], co[2]), 0.0)

    for c in depth_copies:
        c.wait_recv()
    third_tile(lx, l_th[...], [l_co[i] for i in range(4)])

    def wet_rows(i, carry):
        rows = pl.ds(pl.multiple_of(HALO + i * HALO, HALO), HALO)
        for t in range(3):
            mx[t, rows, :] = jnp.where(lx[t, rows, :] > 0.0, 1.0, 0.0)
        return carry

    n_tiles = (EXT - 2 * HALO) // HALO
    for i in range(n_tiles):
        wet_rows(i, 0)

    largest = jnp.zeros((HALO, LANES), F32)
    keep8 = inside(lanes8)
    for i in range(n_tiles):
        r0 = HALO + i * HALO
        rows = pl.ds(r0, HALO)
        sum_m = nine_sum(mx, r0, HALO, lanes8)
        sum_l = nine_sum(lx, r0, HALO, lanes8)
        for t in range(3):
            depth, wet = lx[t, rows, :], mx[t, rows, :]
            diag = 0.5 + 0.125 * (depth * sum_m[t] + wet * sum_l[t])
            if t < 2 and FIRST <= r0 < LAST:
                largest = jnp.maximum(largest, diag)
            recip = 1.0 / diag
            if t == 2:
                recip = jnp.where(keep8, recip, 0.0)
            inv[t, rows, :] = recip
            a1[t, rows, :] = 0.125 * recip * depth
            a2[t, rows, :] = 0.125 * recip * wet
    mine[...] = largest

    across = [
        remote(mine, max_x.at[d], (lax.rem(gx + d, nx), gy)) for d in range(1, nx)
    ]

    for c in field_copies:
        c.wait_recv()
    for f in range(4):
        third_tile(fx.at[f], f_th[f], [f_co[i, f] for i in range(4)])
    for i in range(n_tiles):
        rows = pl.ds(HALO + i * HALO, HALO)
        for t in range(3):
            value = fx[0, t, rows, :]
            ext_ref[0, t, rows, :] = value
            xa[t, rows, :] = mx[t, rows, :] * value
            ya[t, rows, :] = lx[t, rows, :] * value

    def apply(x_ref, y_ref, r0):
        rows = pl.ds(r0, HALO)
        sum_x = nine_sum(x_ref, r0, HALO, lanes8)
        sum_y = nine_sum(y_ref, r0, HALO, lanes8)
        return [a1[t, rows, :] * sum_x[t] + a2[t, rows, :] * sum_y[t] for t in range(3)]

    for i in range(n_tiles):
        r0 = HALO + i * HALO
        rows = pl.ds(r0, HALO)
        moved = apply(xa, ya, r0)
        flux = [fx[3, t, rows, :] for t in range(3)]
        flux_n, flux_s = to_north(flux, lanes8), to_south(flux, lanes8)
        for t in range(3):
            div = fx[2, t, pl.ds(r0 + 1, HALO), :] - fx[2, t, pl.ds(r0 - 1, HALO), :]
            div = div + (flux_n[t] - flux_s[t])
            rhs = fx[1, t, rows, :] - 0.25 * div
            value = inv[t, rows, :] * rhs + (moved[t] - fx[0, t, rows, :])
            zx[t, rows, :] = value
            xb[t, rows, :] = mx[t, rows, :] * value
            yb[t, rows, :] = lx[t, rows, :] * value
    for i in range(n_tiles):
        r0 = HALO + i * HALO
        rows = pl.ds(r0, HALO)
        moved = apply(xb, yb, r0)
        for t in range(3):
            value = zx[t, rows, :] + moved[t]
            ext_ref[1, t, rows, :] = value
            xa[t, rows, :] = mx[t, rows, :] * value
            ya[t, rows, :] = lx[t, rows, :] * value
    for i in range(n_tiles):
        r0 = HALO + i * HALO
        rows = pl.ds(r0, HALO)
        moved = apply(xa, ya, r0)
        for t in range(3):
            xb[t, rows, :] = moved[t]
            yb[t, rows, :] = lx[t, rows, :] * moved[t]
    for i in range(n_tiles):
        r0 = HALO + i * HALO
        rows = pl.ds(r0, HALO)
        moved = apply(xb, yb, r0)
        for t in range(3):
            ext_ref[2, t, rows, :] = moved[t]

    def marks(depth, base):
        count = jnp.clip(depth.astype(I32) - base, 0, 8)
        return jnp.left_shift(jnp.ones_like(count), 3 * count) - 1

    each = 0o11111111
    for i in range(ROWS // HALO):
        r0 = FIRST + i * HALO
        rows = pl.ds(r0, HALO)
        for half in range(2):
            base = 8 * half
            here = [marks(lx[t, rows, :], base) for t in range(3)]
            bits = [h & each for h in here]
            n_bits, s_bits = to_north(bits, lanes8), to_south(bits, lanes8)
            for t in range(2):
                e_bits = marks(lx[t, pl.ds(r0 + 1, HALO), :], base) & each
                w_bits = marks(lx[t, pl.ds(r0 - 1, HALO), :], base) & each
                total = (n_bits[t] + s_bits[t]) + (e_bits + w_bits)
                cnt[half, t, pl.ds(r0 - FIRST, HALO), :] = total & here[t]

    for c in tracer_copies:
        c.wait_recv()
    for plane in range(2 * LEVELS):
        for t in range(2):
            psc[plane, t, pl.ds(HALO - 1, 1), :] = got_w[pl.ds(2 * plane + t, 1), :]
            psc[plane, t, pl.ds(HALO + ROWS, 1), :] = got_e[pl.ds(2 * plane + t, 1), :]
    got_n[...] = jnp.where(gy < ny - 1, got_n[...], 0.0)
    got_s[...] = jnp.where(gy > 0, got_s[...], 0.0)
    c_u.wait()
    c_v.wait()

    lanes16 = lane_ids(CHUNK)

    def tracer_level(k, carry):
        half = k // 8
        shift = 3 * (k - 8 * half)
        level = k.astype(F32)
        for i in range(ROWS // CHUNK):
            r0 = i * CHUNK
            rows = pl.ds(r0, CHUNK)
            coef = []
            for t in range(2):
                lanes = pl.ds(t * LANES, LANES)
                wet = lx[t, pl.ds(FIRST + r0, CHUNK), :] > level
                fifth = jnp.where(wet, 0.2, 0.0)
                quarter = jnp.where(wet, 0.25, 0.0)
                fast_x = us[k, rows, lanes].astype(F32) * quarter
                fast_y = vs[k, rows, lanes].astype(F32) * quarter
                number = jnp.right_shift(cnt[half, t, rows, :], shift) & 7
                centre = 1.0 - 0.2 * number.astype(F32)
                coef.append(
                    (centre, fifth - fast_x, fifth + fast_x, fifth - fast_y, fifth + fast_y)
                )
            for c in range(2):
                plane = c * LEVELS + k
                mid_p = [psc[plane, t, pl.ds(HALO + r0, CHUNK), :] for t in range(2)]
                edge_n = pltpu.roll(got_n[rows, :], LANES - 1 - plane, 1)
                edge_s = pltpu.roll(got_s[rows, :], LANES - plane, 1)
                up = [pltpu.roll(p, LANES - 1, 1) for p in mid_p]
                down = [pltpu.roll(p, 1, 1) for p in mid_p]
                top, bottom = lanes16 == LANES - 1, lanes16 == 0
                north_p = [jnp.where(top, up[1], up[0]), jnp.where(top, edge_n, up[1])]
                south_p = [jnp.where(bottom, edge_s, down[0]), jnp.where(bottom, down[0], down[1])]
                for t in range(2):
                    lanes = pl.ds(t * LANES, LANES)
                    centre, k_e, k_w, k_n, k_s = coef[t]
                    value = centre * trs[c, k, rows, lanes]
                    value = value + k_e * psc[plane, t, pl.ds(HALO + r0 + 1, CHUNK), :]
                    value = value + k_w * psc[plane, t, pl.ds(HALO + r0 - 1, CHUNK), :]
                    out_ref[c, k, rows, lanes] = value + (k_n * north_p[t] + k_s * south_p[t])
        return carry

    lax.fori_loop(0, LEVELS // 2, tracer_level, 0)

    for c in across:
        c.wait_recv()
    largest = mine[...]
    for d in range(1, nx):
        largest = jnp.maximum(largest, max_x[d])
    mid[...] = largest
    along = [
        remote(mid, max_y.at[d], (gx, lax.rem(gy + d, ny))) for d in range(1, ny)
    ]

    lax.fori_loop(LEVELS // 2, LEVELS, tracer_level, 0)

    for c in along:
        c.wait_recv()
    for d in range(1, ny):
        largest = jnp.maximum(largest, max_y[d])
    peak_ref[...] = largest
    for c in depth_copies + field_copies + tracer_copies + across + along:
        c.wait_send()


def finish_kernel(big, ext, own, peak, tr_out, surf_out, tx_out, ty_out, sx, stage, sem, out_sem):
    copies = []
    for c in range(2):
        for q in range(4):
            levels = pl.ds(4 * q, 4)
            copies.append(
                pltpu.make_async_copy(
                    big.at[c, levels], tr_out.at[c, levels], sem.at[4 * c + q]
                )
            )
    for c in copies:
        c.start()
    top = jnp.zeros((HALO, LANES), F32) + jnp.max(peak[...], axis=(0, 1), keepdims=True)
    lowest = 0.5 / top
    scale = 1.0 / (1.0 - lowest)
    four = 4.0 * scale * scale
    w2 = 1.0 / (1.0 - 2.0 / four)
    w3 = 1.0 / (1.0 - w2 / four)
    w4 = 1.0 / (1.0 - w3 / four)
    c0 = 1.0 - (w2 - 1.0) * (w4 - 1.0)
    c2 = w2 * w3 * w4
    for i in range((EXT - 2 * HALO) // HALO):
        rows = pl.ds(HALO + i * HALO, HALO)
        for t in range(3):
            sx[t, rows, :] = ext[0, t, rows, :] + (c0 * ext[1, t, rows, :] + c2 * ext[2, t, rows, :])
    lanes8 = lane_ids(HALO)
    for i in range(ROWS // HALO):
        r0 = FIRST + i * HALO
        rows, dst = pl.ds(r0, HALO), pl.ds(i * HALO, HALO)
        surf = [sx[t, rows, :] for t in range(3)]
        n_val, s_val = to_north(surf, lanes8), to_south(surf, lanes8)
        for t in range(2):
            lanes = pl.ds(t * LANES, LANES)
            wet = 0.25 * own[2, t, dst, :]
            diff = sx[t, pl.ds(r0 + 1, HALO), :] - sx[t, pl.ds(r0 - 1, HALO), :]
            stage[0, dst, lanes] = surf[t]
            stage[1, dst, lanes] = own[0, t, dst, :] - wet * diff
            stage[2, dst, lanes] = own[1, t, dst, :] - wet * (n_val[t] - s_val[t])
    ends = []
    for i, ref in enumerate((surf_out, tx_out, ty_out)):
        ends.append(pltpu.make_async_copy(stage.at[i], ref, out_sem.at[i]))
    for c in ends:
        c.start()
    for c in copies + ends:
        c.wait()


def in_hbm(value):
    return pltpu.with_memory_space_constraint(value, pltpu.HBM)


def local(tracer, zonal, merid, surface, flow_x, flow_y, land_mask, levels):
    nx, ny = lax.axis_size("gx"), lax.axis_size("gy")
    hbm = pl.BlockSpec(memory_space=pltpu.HBM)
    vmem = pl.BlockSpec(memory_space=pltpu.VMEM)
    wide = pltpu.VMEM((3, EXT, LANES), F32)
    n_remote = 20 + (nx - 1) + (ny - 1)
    planes = 2 * LEVELS
    args = (tracer, zonal, merid, surface, flow_x, flow_y, land_mask, levels)
    big, ext, own, peak = pl.pallas_call(
        step_kernel,
        out_shape=(
            pltpu.VMEM((2, LEVELS, ROWS, COLS), F32),
            pltpu.VMEM((3, 3, EXT, LANES), F32),
            pltpu.VMEM((3, 2, ROWS, LANES), F32),
            pltpu.VMEM((HALO, LANES), F32),
        ),
        in_specs=[hbm] * 8,
        out_specs=(vmem,) * 4,
        scratch_shapes=[
            pltpu.VMEM((2, LEVELS, ROWS, COLS), F32),
            pltpu.VMEM((LEVELS, ROWS, COLS), jnp.bfloat16),
            pltpu.VMEM((LEVELS, ROWS, COLS), jnp.bfloat16),
            pltpu.VMEM((2, ROWS, LANES), I32),
            pltpu.VMEM((2, ROWS, LANES), I32),
            pltpu.VMEM((2, 2, ROWS, LANES), F32),
            wide,
            pltpu.VMEM((4, 3, EXT, LANES), F32),
            wide, wide, wide, wide, wide, wide, wide, wide, wide,
            pltpu.VMEM((2, 2, ROWS, LANES), I32),
            pltpu.VMEM((planes, 2, ROWS + 2 * HALO, LANES), F32),
            pltpu.VMEM((2 * planes, LANES), F32),
            pltpu.VMEM((2 * planes, LANES), F32),
            pltpu.VMEM((2 * planes, LANES), F32),
            pltpu.VMEM((2 * planes, LANES), F32),
            pltpu.VMEM((ROWS, LANES), F32),
            pltpu.VMEM((ROWS, LANES), F32),
            pltpu.VMEM((ROWS, LANES), F32),
            pltpu.VMEM((ROWS, LANES), F32),
            pltpu.VMEM((HALO, ROWS), F32),
            pltpu.VMEM((HALO, ROWS), F32),
            pltpu.VMEM((LANES, ROWS), F32),
            pltpu.VMEM((4, HALO, LANES), F32),
            pltpu.VMEM((4, HALO, ROWS), F32),
            pltpu.VMEM((4, HALO, ROWS), F32),
            pltpu.VMEM((4, LANES, ROWS), F32),
            pltpu.VMEM((4, 4, HALO, LANES), F32),
            pltpu.VMEM((HALO, LANES), F32),
            pltpu.VMEM((HALO, LANES), F32),
            pltpu.VMEM((nx, HALO, LANES), F32),
            pltpu.VMEM((ny, HALO, LANES), F32),
            pltpu.SemaphoreType.DMA((10,)),
            pltpu.SemaphoreType.DMA((NGROUPS,)),
            pltpu.SemaphoreType.DMA((2,)),
            pltpu.SemaphoreType.DMA((n_remote,)),
            pltpu.SemaphoreType.DMA((n_remote,)),
        ],
        compiler_params=pltpu.CompilerParams(
            collective_id=1, has_side_effects=True, vmem_limit_bytes=44 << 20
        ),
        name="ocean_step",
    )(*[in_hbm(a) for a in args])
    return pl.pallas_call(
        finish_kernel,
        out_shape=(
            jax.ShapeDtypeStruct((2, LEVELS, ROWS, COLS), F32),
            jax.ShapeDtypeStruct((ROWS, COLS), F32),
            jax.ShapeDtypeStruct((ROWS, COLS), F32),
            jax.ShapeDtypeStruct((ROWS, COLS), F32),
        ),
        in_specs=[vmem] * 4,
        out_specs=(hbm,) * 4,
        scratch_shapes=[
            wide,
            pltpu.VMEM((3, ROWS, COLS), F32),
            pltpu.SemaphoreType.DMA((8,)),
            pltpu.SemaphoreType.DMA((3,)),
        ],
        compiler_params=pltpu.CompilerParams(vmem_limit_bytes=24 << 20),
        name="ocean_finish",
    )(big, ext, own, peak)


def solution(mesh):
    flat = P("gx", "gy")
    deep = P(None, "gx", "gy")
    full = P(None, None, "gx", "gy")
    return jax.shard_map(
        local,
        mesh=mesh,
        in_specs=(full, deep, deep, flat, flat, flat, flat, flat),
        out_specs=(full, flat, flat, flat),
        check_vma=False,
    )
```

```python
import jax
import jax.numpy as jnp
from jax import lax
from jax.experimental import pallas as pl
from jax.experimental.pallas import tpu as pltpu
from jax.sharding import PartitionSpec as P

MESH = pl.DeviceIdType.MESH
F32 = jnp.float32
I32 = jnp.int32

LEVELS = 16
ROWS = 224
COLS = 256
LANES = 128
HALO = 8
FIRST = 16
LAST = FIRST + ROWS
EXT = 256
GROUP = 32
NGROUPS = ROWS // GROUP
CHUNK = 16
NCHUNKS = ROWS // CHUNK
EARLY_GROUPS = 2
FIRST_CHUNKS = 2
STEP_CHUNKS = 11


def lane_ids(rows):
    return lax.broadcasted_iota(I32, (rows, LANES), 1)


def to_north(tiles, lanes):
    moved = [pltpu.roll(t, LANES - 1, 1) for t in tiles]
    n = len(tiles)
    return [jnp.where(lanes == LANES - 1, moved[(i + 1) % n], moved[i]) for i in range(n)]


def to_south(tiles, lanes):
    moved = [pltpu.roll(t, 1, 1) for t in tiles]
    n = len(tiles)
    return [jnp.where(lanes == 0, moved[(i - 1) % n], moved[i]) for i in range(n)]


def nine_sum(ref, r0, rows, lanes):
    sides, inner = [], []
    for t in range(3):
        here = ref[t, pl.ds(r0, rows), :]
        pair = ref[t, pl.ds(r0 + 1, rows), :] + ref[t, pl.ds(r0 - 1, rows), :]
        sides.append(pair)
        inner.append(here + 0.5 * pair)
    north = to_north(inner, lanes)
    south = to_south(inner, lanes)
    return [sides[t] + (north[t] + south[t]) for t in range(3)]


def tracer_chunk(i, trs, us, vs, psc, own, cnt, edge, out, out_row):
    lanes16 = lane_ids(CHUNK)
    top, bottom = lanes16 == LANES - 1, lanes16 == 0
    r0 = pl.multiple_of(i * CHUNK, CHUNK)
    rows = pl.ds(r0, CHUNK)
    halo = r0 + HALO
    beside = edge[rows, :]
    depth = [own[2, t, rows, :] for t in range(2)]
    for k in range(LEVELS):
        half, shift = k // 8, 3 * (k % 8)
        coef = []
        for t in range(2):
            lanes = pl.ds(t * LANES, LANES)
            wet = depth[t] > float(k)
            fifth = jnp.where(wet, 0.2, 0.0)
            quarter = jnp.where(wet, 0.25, 0.0)
            fast_x = us[k, rows, lanes].astype(F32) * quarter
            fast_y = vs[k, rows, lanes].astype(F32) * quarter
            number = jnp.right_shift(cnt[half, t, rows, :], shift) & 7
            centre = 1.0 - 0.2 * number.astype(F32)
            coef.append((centre, fifth - fast_x, fifth + fast_x, fifth - fast_y, fifth + fast_y))
        for c in range(2):
            plane = c * LEVELS + k
            here = [psc[plane, t, pl.ds(halo, CHUNK), :] for t in range(2)]
            ends = pltpu.roll(beside, LANES - 1 - 2 * plane, 1)
            up = [pltpu.roll(p, LANES - 1, 1) for p in here]
            down = [pltpu.roll(p, 1, 1) for p in here]
            north_p = [jnp.where(top, up[1], up[0]), jnp.where(top, ends, up[1])]
            south_p = [jnp.where(bottom, ends, down[0]), jnp.where(bottom, down[0], down[1])]
            for t in range(2):
                lanes = pl.ds(t * LANES, LANES)
                centre, k_e, k_w, k_n, k_s = coef[t]
                value = centre * trs[c, k, rows, lanes]
                value = value + k_e * psc[plane, t, pl.ds(halo + 1, CHUNK), :]
                value = value + k_w * psc[plane, t, pl.ds(halo - 1, CHUNK), :]
                out[c, k, pl.ds(out_row, CHUNK), lanes] = value + (
                    k_n * north_p[t] + k_s * south_p[t]
                )


def step_kernel(
    tr_hbm, u_hbm, v_hbm, e0_hbm, tx_hbm, ty_hbm, mask_hbm, lev_hbm,
    out_ref, ext_ref, own_ref, peak_ref, trs, us, vs, psc, cnt, edge,
    mask_s, lev_s, raw_s,
    lx, fx, mx, a1, a2, inv, xa, ya, xb, yb, zx,
    row_e, row_w, got_e, got_w, pack, turned_p, col_n, col_s, got_n, got_s,
    l_n, l_s, l_th, l_co, f_n, f_s, f_th, f_co,
    mine, mid, max_x, max_y,
    in_sem, tr_sem, uv_sem, send_sem, recv_sem,
):
    gx = lax.axis_index("gx")
    gy = lax.axis_index("gy")
    nx, ny = 16, 8
    east, west = lax.rem(gx + 1, nx), lax.rem(gx + nx - 1, nx)
    north, south = lax.rem(gy + 1, ny), lax.rem(gy + ny - 1, ny)
    corners = ((east, north), (east, south), (west, north), (west, south))
    ring, x_hi, core = gx // 4, lax.rem(gx // 2, 2), lax.rem(gx, 2)
    plane_mates = [
        (ring * 4 + lax.rem(x_hi + d // 8, 2) * 2 + core, lax.rem(gy + d % 8, ny))
        for d in range(1, 16)
    ]
    line_mates = [
        (lax.rem(ring + d % 4, 4) * 4 + x_hi * 2 + lax.rem(core + d // 4, 2), gy)
        for d in range(1, 8)
    ]
    sides = ((east, gy), (west, gy), (gx, north), (gx, south))

    barrier = pltpu.get_barrier_semaphore()
    greeted = (*plane_mates, *line_mates, *sides, *corners)
    for mate in greeted:
        pl.semaphore_signal(barrier, inc=1, device_id=mate, device_id_type=MESH)

    def flat_copy(src, dst, slot):
        copies = []
        for t in range(2):
            copies.append(
                pltpu.make_async_copy(
                    src.at[:, pl.ds(t * LANES, LANES)], dst(t), in_sem.at[2 * slot + t]
                )
            )
        for c in copies:
            c.start()
        return copies

    c_mask = flat_copy(mask_hbm, lambda t: mask_s.at[t], 0)
    c_lev = flat_copy(lev_hbm, lambda t: lev_s.at[t], 1)
    c_tx = flat_copy(tx_hbm, lambda t: raw_s.at[0, t], 2)
    c_ty = flat_copy(ty_hbm, lambda t: raw_s.at[1, t], 3)
    c_e0 = flat_copy(e0_hbm, lambda t: fx.at[0, t, pl.ds(FIRST, ROWS), :], 4)

    def group_copy(g):
        rows = pl.ds(pl.multiple_of(g * GROUP, GROUP), GROUP)
        return pltpu.make_async_copy(
            tr_hbm.at[:, :, rows, :], trs.at[:, :, rows, :], tr_sem.at[g]
        )

    for g in range(NGROUPS):
        group_copy(g).start()
    c_u = pltpu.make_async_copy(u_hbm, us, uv_sem.at[0])
    c_v = pltpu.make_async_copy(v_hbm, vs, uv_sem.at[1])

    for ref in (mx, lx, xa, ya, xb, yb):
        for t in range(3):
            ref[t, pl.ds(0, HALO), :] = jnp.zeros((HALO, LANES), F32)
            ref[t, pl.ds(EXT - HALO, HALO), :] = jnp.zeros((HALO, LANES), F32)

    pack[pl.ds(ROWS, 2 * LANES - ROWS), :] = jnp.zeros((2 * LANES - ROWS, LANES), F32)

    for c in c_mask + c_lev:
        c.wait()
    for t in range(2):
        depth = (lev_s[t] * mask_s[t]).astype(F32)
        lx[t, pl.ds(FIRST, ROWS), :] = depth
        own_ref[2, t] = depth
        mx[t, pl.ds(FIRST, ROWS), :] = jnp.where(depth > 0.0, 1.0, 0.0)
        turned = jnp.transpose(depth)
        if t == 0:
            l_s[...] = turned[:HALO]
        else:
            l_n[...] = turned[LANES - HALO :]
    for c in c_tx + c_ty + c_e0:
        c.wait()
    for t in range(2):
        wet = lx[t, pl.ds(FIRST, ROWS), :] > 0.0
        for i in range(2):
            value = jnp.where(wet, raw_s[i, t], 0.0)
            own_ref[i, t] = value
            fx[1 + i, t, pl.ds(FIRST, ROWS), :] = value

    def turn_edges(f):
        f_s[f] = jnp.transpose(fx[f, 0, pl.ds(FIRST, ROWS), :])[:HALO]
        f_n[f] = jnp.transpose(fx[f, 1, pl.ds(FIRST, ROWS), :])[LANES - HALO :]

    for f in range(3):
        turn_edges(f)

    glanes = lane_ids(GROUP)

    def force_group(g, carry):
        group_copy(g).wait()
        r0 = pl.multiple_of(g * GROUP, GROUP)
        depth = [lx[t, pl.ds(r0 + FIRST, GROUP), :] for t in range(2)]
        total = [jnp.zeros((GROUP, LANES), F32) for _ in range(2)]
        cols = jnp.zeros((GROUP, LANES), F32)
        for k in range(LEVELS):
            kept = {}
            for t in range(2):
                lanes = pl.ds(t * LANES, LANES)
                left = depth[t] - float(k)
                wet = left > 0.0
                t0 = trs[0, k, pl.ds(r0, GROUP), lanes]
                t1 = trs[1, k, pl.ds(r0, GROUP), lanes]
                total[t] = total[t] + jnp.maximum(left, 0.0) * (0.8 * t0 - 0.6 * t1)
                for i, value in enumerate((t0, t1)):
                    plane = i * LEVELS + k
                    value = jnp.where(wet, value, 0.0)
                    psc[plane, t, pl.ds(r0 + HALO, GROUP), :] = value
                    kept[t, i] = value
            for i in range(2):
                lane = 2 * (i * LEVELS + k)
                moved = pltpu.roll(jnp.where(glanes == 0, kept[0, i], kept[1, i]), lane + 1, 1)
                cols = jnp.where((glanes >= lane) & (glanes <= lane + 1), moved, cols)
        pack[pl.ds(r0, GROUP), :] = cols
        for t in range(2):
            rows = pl.ds(r0 + FIRST, GROUP)
            fx[3, t, rows, :] = total[t] * (1.0 / LEVELS) + 0.5 * fx[0, t, rows, :]
        return carry

    lax.fori_loop(0, EARLY_GROUPS, force_group, 0)
    c_u.start()
    c_v.start()

    pl.semaphore_wait(barrier, len(greeted))

    started = [0]

    def remote(src, dst, who):
        slot = started[0]
        started[0] += 1
        copy = pltpu.make_async_remote_copy(
            src_ref=src,
            dst_ref=dst,
            send_sem=send_sem.at[slot],
            recv_sem=recv_sem.at[slot],
            device_id=who,
            device_id_type=MESH,
        )
        copy.start()
        return copy

    high, low = pl.ds(LAST - HALO, HALO), pl.ds(FIRST, HALO)
    below, above = pl.ds(FIRST - HALO, HALO), pl.ds(LAST, HALO)
    both = pl.ds(0, 2)
    depth_copies = [
        remote(lx.at[1, high, :], l_co.at[0], (east, north)),
        remote(lx.at[0, high, :], l_co.at[1], (east, south)),
        remote(lx.at[1, low, :], l_co.at[2], (west, north)),
        remote(lx.at[0, low, :], l_co.at[3], (west, south)),
        remote(lx.at[both, high, :], lx.at[both, below, :], (east, gy)),
        remote(lx.at[both, low, :], lx.at[both, above, :], (west, gy)),
        remote(l_n, l_th.at[pl.ds(LANES - HALO, HALO), :], (gx, north)),
        remote(l_s, l_th.at[pl.ds(0, HALO), :], (gx, south)),
    ]

    def send_fields(which):
        return [
            remote(fx.at[which, both, high, :], fx.at[which, both, below, :], (east, gy)),
            remote(fx.at[which, both, low, :], fx.at[which, both, above, :], (west, gy)),
            remote(f_n.at[which], f_th.at[which, pl.ds(LANES - HALO, HALO), :], (gx, north)),
            remote(f_s.at[which], f_th.at[which, pl.ds(0, HALO), :], (gx, south)),
            remote(fx.at[which, 1, high, :], f_co.at[0, which], (east, north)),
            remote(fx.at[which, 0, high, :], f_co.at[1, which], (east, south)),
            remote(fx.at[which, 1, low, :], f_co.at[2, which], (west, north)),
            remote(fx.at[which, 0, low, :], f_co.at[3, which], (west, south)),
        ]

    field_copies = send_fields(pl.ds(0, 3))

    lax.fori_loop(EARLY_GROUPS, NGROUPS, force_group, 0)
    for plane in range(2 * LEVELS):
        for t in range(2):
            row_w[pl.ds(2 * plane + t, 1), :] = psc[plane, t, pl.ds(HALO, 1), :]
            row_e[pl.ds(2 * plane + t, 1), :] = psc[plane, t, pl.ds(HALO + ROWS - 1, 1), :]
    planes = 2 * LEVELS
    for h in range(2):
        turned_p[h] = jnp.transpose(pack[pl.ds(h * LANES, LANES), :])
        col_n[h] = turned_p[h, pl.ds(0, planes, stride=2), :]
        col_s[h] = turned_p[h, pl.ds(1, planes, stride=2), :]
    tracer_copies = [
        remote(row_e, got_w, (east, gy)),
        remote(row_w, got_e, (west, gy)),
        remote(col_n, got_s, (gx, north)),
        remote(col_s, got_n, (gx, south)),
    ]
    turn_edges(3)
    force_copies = send_fields(pl.ds(3, 1))

    lanes8 = lane_ids(HALO)
    lanes_all = lane_ids(ROWS)

    def inside(lanes):
        return ((lanes < HALO) & (gy < ny - 1)) | ((lanes >= LANES - HALO) & (gy > 0))

    def third_tile(dst, turned, co):
        keep8 = inside(lanes8)
        dst[2, pl.ds(FIRST, ROWS), :] = jnp.where(inside(lanes_all), jnp.transpose(turned), 0.0)
        dst[2, below, :] = jnp.where(keep8, jnp.where(lanes8 < HALO, co[1], co[0]), 0.0)
        dst[2, above, :] = jnp.where(keep8, jnp.where(lanes8 < HALO, co[3], co[2]), 0.0)

    for c in depth_copies:
        c.wait_recv()
    third_tile(lx, l_th[...], [l_co[i] for i in range(4)])

    n_tiles = (EXT - 2 * HALO) // HALO
    for i in range(n_tiles):
        rows = pl.ds(HALO + i * HALO, HALO)
        for t in range(3):
            if t == 2 or i == 0 or i == n_tiles - 1:
                mx[t, rows, :] = jnp.where(lx[t, rows, :] > 0.0, 1.0, 0.0)

    largest = jnp.zeros((HALO, LANES), F32)
    for i in range(n_tiles):
        r0 = HALO + i * HALO
        rows = pl.ds(r0, HALO)
        sum_m = nine_sum(mx, r0, HALO, lanes8)
        sum_l = nine_sum(lx, r0, HALO, lanes8)
        for t in range(3):
            value = 0.5 + 0.125 * (lx[t, rows, :] * sum_m[t] + mx[t, rows, :] * sum_l[t])
            inv[t, rows, :] = value
            if t < 2 and FIRST <= r0 < LAST:
                largest = jnp.maximum(largest, value)
    mine[...] = largest

    across = [remote(mine, max_x.at[d], mate) for d, mate in enumerate(plane_mates)]

    keep8 = inside(lanes8)
    for i in range(n_tiles):
        rows = pl.ds(HALO + i * HALO, HALO)
        for t in range(3):
            recip = 1.0 / inv[t, rows, :]
            if t == 2:
                recip = jnp.where(keep8, recip, 0.0)
            inv[t, rows, :] = recip
            eighth = 0.125 * recip
            a1[t, rows, :] = eighth * lx[t, rows, :]
            a2[t, rows, :] = eighth * mx[t, rows, :]

    for c in field_copies:
        c.wait_recv()
    for f in range(3):
        third_tile(fx.at[f], f_th[f], [f_co[i, f] for i in range(4)])
    for i in range(n_tiles):
        rows = pl.ds(HALO + i * HALO, HALO)
        for t in range(3):
            value = fx[0, t, rows, :]
            ext_ref[0, t, rows, :] = value
            xa[t, rows, :] = mx[t, rows, :] * value
            ya[t, rows, :] = lx[t, rows, :] * value

    def apply(x_ref, y_ref, r0):
        rows = pl.ds(r0, HALO)
        sum_x = nine_sum(x_ref, r0, HALO, lanes8)
        sum_y = nine_sum(y_ref, r0, HALO, lanes8)
        return [a1[t, rows, :] * sum_x[t] + a2[t, rows, :] * sum_y[t] for t in range(3)]

    for i in range(n_tiles):
        r0 = HALO + i * HALO
        rows = pl.ds(r0, HALO)
        moved = apply(xa, ya, r0)
        flux = [fx[2, t, rows, :] for t in range(3)]
        flux_n, flux_s = to_north(flux, lanes8), to_south(flux, lanes8)
        for t in range(3):
            div = fx[1, t, pl.ds(r0 + 1, HALO), :] - fx[1, t, pl.ds(r0 - 1, HALO), :]
            div = div + (flux_n[t] - flux_s[t])
            zx[t, rows, :] = (moved[t] - fx[0, t, rows, :]) - 0.25 * inv[t, rows, :] * div

    def marks(depth, base):
        count = jnp.clip(depth.astype(I32) - base, 0, 8)
        return jnp.left_shift(jnp.ones_like(count), 3 * count) - 1

    each = 0o11111111
    for i in range(ROWS // HALO):
        r0 = FIRST + i * HALO
        rows = pl.ds(r0, HALO)
        for half in range(2):
            base = 8 * half
            here = [marks(lx[t, rows, :], base) for t in range(3)]
            bits = [h & each for h in here]
            n_bits, s_bits = to_north(bits, lanes8), to_south(bits, lanes8)
            for t in range(2):
                e_bits = marks(lx[t, pl.ds(r0 + 1, HALO), :], base) & each
                w_bits = marks(lx[t, pl.ds(r0 - 1, HALO), :], base) & each
                total = (n_bits[t] + s_bits[t]) + (e_bits + w_bits)
                cnt[half, t, pl.ds(r0 - FIRST, HALO), :] = total & here[t]

    for c in force_copies:
        c.wait_recv()
    third_tile(fx.at[3], f_th[3], [f_co[i, 3] for i in range(4)])
    for i in range(n_tiles):
        rows = pl.ds(HALO + i * HALO, HALO)
        for t in range(3):
            value = zx[t, rows, :] + inv[t, rows, :] * fx[3, t, rows, :]
            zx[t, rows, :] = value
            xb[t, rows, :] = mx[t, rows, :] * value
            yb[t, rows, :] = lx[t, rows, :] * value
    for i in range(n_tiles):
        r0 = HALO + i * HALO
        rows = pl.ds(r0, HALO)
        moved = apply(xb, yb, r0)
        for t in range(3):
            value = zx[t, rows, :] + moved[t]
            ext_ref[1, t, rows, :] = value
            xa[t, rows, :] = mx[t, rows, :] * value
            ya[t, rows, :] = lx[t, rows, :] * value
    for i in range(n_tiles):
        r0 = HALO + i * HALO
        rows = pl.ds(r0, HALO)
        moved = apply(xa, ya, r0)
        for t in range(3):
            xb[t, rows, :] = moved[t]
            yb[t, rows, :] = lx[t, rows, :] * moved[t]
    for i in range(n_tiles):
        r0 = HALO + i * HALO
        rows = pl.ds(r0, HALO)
        moved = apply(xb, yb, r0)
        for t in range(3):
            ext_ref[2, t, rows, :] = moved[t]

    for c in tracer_copies:
        c.wait_recv()
    for plane in range(2 * LEVELS):
        for t in range(2):
            psc[plane, t, pl.ds(HALO - 1, 1), :] = got_w[pl.ds(2 * plane + t, 1), :]
            psc[plane, t, pl.ds(HALO + ROWS, 1), :] = got_e[pl.ds(2 * plane + t, 1), :]
    for h in range(2):
        turned_p[h, pl.ds(0, planes, stride=2), :] = jnp.where(gy < ny - 1, got_n[h], 0.0)
        turned_p[h, pl.ds(1, planes, stride=2), :] = jnp.where(gy > 0, got_s[h], 0.0)
        edge[pl.ds(h * LANES, LANES), :] = jnp.transpose(turned_p[h])
    c_u.wait()
    c_v.wait()

    def step_chunk(i, carry):
        row = pl.multiple_of(i * CHUNK, CHUNK)
        tracer_chunk(i, trs, us, vs, psc, own_ref, cnt, edge, out_ref, row)
        return carry

    lax.fori_loop(0, FIRST_CHUNKS, step_chunk, 0)

    for c in across:
        c.wait_recv()
    largest = mine[...]
    for d in range(len(across)):
        largest = jnp.maximum(largest, max_x[d])
    mid[...] = largest
    along = [remote(mid, max_y.at[d], mate) for d, mate in enumerate(line_mates)]

    lax.fori_loop(FIRST_CHUNKS, STEP_CHUNKS, step_chunk, 0)

    for c in along:
        c.wait_recv()
    for d in range(len(along)):
        largest = jnp.maximum(largest, max_y[d])
    peak_ref[...] = largest
    for c in depth_copies + field_copies + tracer_copies + force_copies + across + along:
        c.wait_send()


def finish_kernel(
    big, ext, own, peak, trs, us, vs, psc, cnt, edge,
    tr_out, surf_out, tx_out, ty_out,
    sx, stage, late, sem, late_sem, out_sem,
):
    copies = []
    done = pl.ds(0, STEP_CHUNKS * CHUNK)
    for c in range(2):
        for q in range(4):
            levels = pl.ds(4 * q, 4)
            copies.append(
                pltpu.make_async_copy(
                    big.at[c, levels], tr_out.at[c, levels, done, :], sem.at[4 * c + q]
                )
            )
    for c in copies:
        c.start()

    def late_copy(i):
        row = pl.multiple_of(i * CHUNK, CHUNK)
        left = pl.multiple_of(row - STEP_CHUNKS * CHUNK, CHUNK)
        return pltpu.make_async_copy(
            late.at[:, :, pl.ds(left, CHUNK), :],
            tr_out.at[:, :, pl.ds(row, CHUNK), :],
            late_sem.at[i - STEP_CHUNKS],
        )

    def late_chunk(i, carry):
        left = pl.multiple_of((i - STEP_CHUNKS) * CHUNK, CHUNK)
        tracer_chunk(i, trs, us, vs, psc, own, cnt, edge, late, left)
        late_copy(i).start()
        return carry

    lax.fori_loop(STEP_CHUNKS, NCHUNKS, late_chunk, 0)
    top = jnp.zeros((HALO, LANES), F32) + jnp.max(peak[...], axis=(0, 1), keepdims=True)
    lowest = 0.5 / top
    scale = 1.0 / (1.0 - lowest)
    four = 4.0 * scale * scale
    w2 = 1.0 / (1.0 - 2.0 / four)
    w3 = 1.0 / (1.0 - w2 / four)
    w4 = 1.0 / (1.0 - w3 / four)
    c0 = 1.0 - (w2 - 1.0) * (w4 - 1.0)
    c2 = w2 * w3 * w4
    for i in range((EXT - 2 * HALO) // HALO):
        rows = pl.ds(HALO + i * HALO, HALO)
        for t in range(3):
            sx[t, rows, :] = ext[0, t, rows, :] + (c0 * ext[1, t, rows, :] + c2 * ext[2, t, rows, :])
    lanes8 = lane_ids(HALO)
    for i in range(ROWS // HALO):
        r0 = FIRST + i * HALO
        rows, dst = pl.ds(r0, HALO), pl.ds(i * HALO, HALO)
        surf = [sx[t, rows, :] for t in range(3)]
        n_val, s_val = to_north(surf, lanes8), to_south(surf, lanes8)
        for t in range(2):
            lanes = pl.ds(t * LANES, LANES)
            wet = jnp.where(own[2, t, dst, :] > 0.0, 0.25, 0.0)
            diff = sx[t, pl.ds(r0 + 1, HALO), :] - sx[t, pl.ds(r0 - 1, HALO), :]
            stage[0, dst, lanes] = surf[t]
            stage[1, dst, lanes] = own[0, t, dst, :] - wet * diff
            stage[2, dst, lanes] = own[1, t, dst, :] - wet * (n_val[t] - s_val[t])
    ends = []
    for i, ref in enumerate((surf_out, tx_out, ty_out)):
        ends.append(pltpu.make_async_copy(stage.at[i], ref, out_sem.at[i]))
    for c in ends:
        c.start()
    for c in copies + ends:
        c.wait()
    for i in range(STEP_CHUNKS, NCHUNKS):
        late_copy(i).wait()


def in_hbm(value):
    return pltpu.with_memory_space_constraint(value, pltpu.HBM)


def local(tracer, zonal, merid, surface, flow_x, flow_y, land_mask, levels):
    hbm = pl.BlockSpec(memory_space=pltpu.HBM)
    vmem = pl.BlockSpec(memory_space=pltpu.VMEM)
    wide = pltpu.VMEM((3, EXT, LANES), F32)
    n_remote = 28 + 15 + 7
    planes = 2 * LEVELS
    left = ROWS - STEP_CHUNKS * CHUNK
    args = (tracer, zonal, merid, surface, flow_x, flow_y, land_mask, levels)
    kept = pl.pallas_call(
        step_kernel,
        out_shape=(
            pltpu.VMEM((2, LEVELS, STEP_CHUNKS * CHUNK, COLS), F32),
            pltpu.VMEM((3, 3, EXT, LANES), F32),
            pltpu.VMEM((3, 2, ROWS, LANES), F32),
            pltpu.VMEM((HALO, LANES), F32),
            pltpu.VMEM((2, LEVELS, ROWS, COLS), F32),
            pltpu.VMEM((LEVELS, ROWS, COLS), jnp.bfloat16),
            pltpu.VMEM((LEVELS, ROWS, COLS), jnp.bfloat16),
            pltpu.VMEM((planes, 2, ROWS + 2 * HALO, LANES), F32),
            pltpu.VMEM((2, 2, ROWS, LANES), I32),
            pltpu.VMEM((2 * LANES, LANES), F32),
        ),
        in_specs=[hbm] * 8,
        out_specs=(vmem,) * 10,
        scratch_shapes=[
            pltpu.VMEM((2, ROWS, LANES), I32),
            pltpu.VMEM((2, ROWS, LANES), I32),
            pltpu.VMEM((2, 2, ROWS, LANES), F32),
            wide,
            pltpu.VMEM((4, 3, EXT, LANES), F32),
            wide, wide, wide, wide, wide, wide, wide, wide, wide,
            pltpu.VMEM((2 * planes, LANES), F32),
            pltpu.VMEM((2 * planes, LANES), F32),
            pltpu.VMEM((2 * planes, LANES), F32),
            pltpu.VMEM((2 * planes, LANES), F32),
            pltpu.VMEM((2 * LANES, LANES), F32),
            pltpu.VMEM((2, LANES, LANES), F32),
            pltpu.VMEM((2, planes, LANES), F32),
            pltpu.VMEM((2, planes, LANES), F32),
            pltpu.VMEM((2, planes, LANES), F32),
            pltpu.VMEM((2, planes, LANES), F32),
            pltpu.VMEM((HALO, ROWS), F32),
            pltpu.VMEM((HALO, ROWS), F32),
            pltpu.VMEM((LANES, ROWS), F32),
            pltpu.VMEM((4, HALO, LANES), F32),
            pltpu.VMEM((4, HALO, ROWS), F32),
            pltpu.VMEM((4, HALO, ROWS), F32),
            pltpu.VMEM((4, LANES, ROWS), F32),
            pltpu.VMEM((4, 4, HALO, LANES), F32),
            pltpu.VMEM((HALO, LANES), F32),
            pltpu.VMEM((HALO, LANES), F32),
            pltpu.VMEM((15, HALO, LANES), F32),
            pltpu.VMEM((7, HALO, LANES), F32),
            pltpu.SemaphoreType.DMA((10,)),
            pltpu.SemaphoreType.DMA((NGROUPS,)),
            pltpu.SemaphoreType.DMA((2,)),
            pltpu.SemaphoreType.DMA((n_remote,)),
            pltpu.SemaphoreType.DMA((n_remote,)),
        ],
        compiler_params=pltpu.CompilerParams(
            collective_id=1, has_side_effects=True, vmem_limit_bytes=20 << 20
        ),
        name="ocean_step",
    )(*[in_hbm(a) for a in args])
    return pl.pallas_call(
        finish_kernel,
        out_shape=(
            jax.ShapeDtypeStruct((2, LEVELS, ROWS, COLS), F32),
            jax.ShapeDtypeStruct((ROWS, COLS), F32),
            jax.ShapeDtypeStruct((ROWS, COLS), F32),
            jax.ShapeDtypeStruct((ROWS, COLS), F32),
        ),
        in_specs=[vmem] * 10,
        out_specs=(hbm,) * 4,
        scratch_shapes=[
            wide,
            pltpu.VMEM((3, ROWS, COLS), F32),
            pltpu.VMEM((2, LEVELS, left, COLS), F32),
            pltpu.SemaphoreType.DMA((8,)),
            pltpu.SemaphoreType.DMA((left // CHUNK,)),
            pltpu.SemaphoreType.DMA((3,)),
        ],
        compiler_params=pltpu.CompilerParams(vmem_limit_bytes=20 << 20),
        name="ocean_finish",
    )(*kept)


def solution(mesh):
    flat = P("gx", "gy")
    deep = P(None, "gx", "gy")
    full = P(None, None, "gx", "gy")
    return jax.shard_map(
        local,
        mesh=mesh,
        in_specs=(full, deep, deep, flat, flat, flat, flat, flat),
        out_specs=(full, flat, flat, flat),
        check_vma=False,
    )
```

```python
import jax
import jax.numpy as jnp
from jax import lax
from jax.experimental import pallas as pl
from jax.experimental.pallas import tpu as pltpu
from jax.sharding import PartitionSpec as P

MESH = pl.DeviceIdType.MESH
F32 = jnp.float32
I32 = jnp.int32

LEVELS = 16
ROWS = 224
COLS = 256
LANES = 128
HALO = 8
FIRST = 16
LAST = FIRST + ROWS
EXT = 256
GROUP = 32
NGROUPS = ROWS // GROUP
CHUNK = 16
NCHUNKS = ROWS // CHUNK
EARLY_GROUPS = 1
FIRST_CHUNKS = 2
STEP_CHUNKS = 11


def lane_ids(rows):
    return lax.broadcasted_iota(I32, (rows, LANES), 1)


def to_north(tiles, lanes):
    moved = [pltpu.roll(t, LANES - 1, 1) for t in tiles]
    n = len(tiles)
    return [jnp.where(lanes == LANES - 1, moved[(i + 1) % n], moved[i]) for i in range(n)]


def to_south(tiles, lanes):
    moved = [pltpu.roll(t, 1, 1) for t in tiles]
    n = len(tiles)
    return [jnp.where(lanes == 0, moved[(i - 1) % n], moved[i]) for i in range(n)]


def nine_sum(ref, r0, rows, lanes):
    sides, inner = [], []
    for t in range(3):
        here = ref[t, pl.ds(r0, rows), :]
        pair = ref[t, pl.ds(r0 + 1, rows), :] + ref[t, pl.ds(r0 - 1, rows), :]
        sides.append(pair)
        inner.append(here + 0.5 * pair)
    north = to_north(inner, lanes)
    south = to_south(inner, lanes)
    return [sides[t] + (north[t] + south[t]) for t in range(3)]


def tracer_chunk(i, trs, us, vs, psc, own, cnt, edge, out, out_row):
    lanes16 = lane_ids(CHUNK)
    top, bottom = lanes16 == LANES - 1, lanes16 == 0
    r0 = pl.multiple_of(i * CHUNK, CHUNK)
    rows = pl.ds(r0, CHUNK)
    halo = r0 + HALO
    beside = edge[rows, :]
    depth = [own[2, t, rows, :] for t in range(2)]
    for k in range(LEVELS):
        half, shift = k // 8, 3 * (k % 8)
        coef = []
        for t in range(2):
            lanes = pl.ds(t * LANES, LANES)
            wet = depth[t] > float(k)
            fifth = jnp.where(wet, 0.2, 0.0)
            quarter = jnp.where(wet, 0.25, 0.0)
            fast_x = us[k, rows, lanes].astype(F32) * quarter
            fast_y = vs[k, rows, lanes].astype(F32) * quarter
            number = jnp.right_shift(cnt[half, t, rows, :], shift) & 7
            centre = 1.0 - 0.2 * number.astype(F32)
            coef.append((centre, fifth - fast_x, fifth + fast_x, fifth - fast_y, fifth + fast_y))
        for c in range(2):
            plane = c * LEVELS + k
            here = [psc[plane, t, pl.ds(halo, CHUNK), :] for t in range(2)]
            ends = pltpu.roll(beside, LANES - 1 - 2 * plane, 1)
            up = [pltpu.roll(p, LANES - 1, 1) for p in here]
            down = [pltpu.roll(p, 1, 1) for p in here]
            north_p = [jnp.where(top, up[1], up[0]), jnp.where(top, ends, up[1])]
            south_p = [jnp.where(bottom, ends, down[0]), jnp.where(bottom, down[0], down[1])]
            for t in range(2):
                lanes = pl.ds(t * LANES, LANES)
                centre, k_e, k_w, k_n, k_s = coef[t]
                value = centre * trs[c, k, rows, lanes]
                value = value + k_e * psc[plane, t, pl.ds(halo + 1, CHUNK), :]
                value = value + k_w * psc[plane, t, pl.ds(halo - 1, CHUNK), :]
                out[c, k, pl.ds(out_row, CHUNK), lanes] = value + (
                    k_n * north_p[t] + k_s * south_p[t]
                )


def step_kernel(
    tr_hbm, u_hbm, v_hbm, e0_hbm, tx_hbm, ty_hbm, mask_hbm, lev_hbm,
    out_ref, ext_ref, own_ref, peak_ref, trs, us, vs, psc, cnt, edge,
    mask_s, lev_s, raw_s,
    lx, fx, mx, a1, a2, inv, xa, ya, xb, yb, zx,
    row_e, row_w, got_e, got_w, pack, turned_p, col_n, col_s, got_n, got_s,
    l_n, l_s, l_th, l_co, f_n, f_s, f_th, f_co,
    mine, mid, max_x, max_y,
    in_sem, tr_sem, uv_sem, send_sem, recv_sem,
):
    gx = lax.axis_index("gx")
    gy = lax.axis_index("gy")
    nx, ny = 16, 8
    east, west = lax.rem(gx + 1, nx), lax.rem(gx + nx - 1, nx)
    north, south = lax.rem(gy + 1, ny), lax.rem(gy + ny - 1, ny)
    corners = ((east, north), (east, south), (west, north), (west, south))
    ring, x_hi, core = gx // 4, lax.rem(gx // 2, 2), lax.rem(gx, 2)
    plane_mates = [
        (ring * 4 + lax.rem(x_hi + d // 8, 2) * 2 + core, lax.rem(gy + d % 8, ny))
        for d in range(1, 16)
    ]
    line_mates = [
        (lax.rem(ring + d % 4, 4) * 4 + x_hi * 2 + lax.rem(core + d // 4, 2), gy)
        for d in range(1, 8)
    ]
    sides = ((east, gy), (west, gy))

    barrier = pltpu.get_barrier_semaphore()
    plane_order = (9, 13, 8, 10, 12, 14, 7, 11, 1, 5, 0, 2, 4, 6, 3)
    greeted = (*corners, *sides, *[plane_mates[d] for d in plane_order], *line_mates)
    for mate in greeted:
        pl.semaphore_signal(barrier, inc=1, device_id=mate, device_id_type=MESH)

    def flat_copy(src, dst, slot):
        copies = []
        for t in range(2):
            copies.append(
                pltpu.make_async_copy(
                    src.at[:, pl.ds(t * LANES, LANES)], dst(t), in_sem.at[2 * slot + t]
                )
            )
        for c in copies:
            c.start()
        return copies

    c_mask = flat_copy(mask_hbm, lambda t: mask_s.at[t], 0)
    c_lev = flat_copy(lev_hbm, lambda t: lev_s.at[t], 1)
    c_tx = flat_copy(tx_hbm, lambda t: raw_s.at[0, t], 2)
    c_ty = flat_copy(ty_hbm, lambda t: raw_s.at[1, t], 3)
    c_e0 = flat_copy(e0_hbm, lambda t: fx.at[0, t, pl.ds(FIRST, ROWS), :], 4)

    def group_copy(g):
        rows = pl.ds(pl.multiple_of(g * GROUP, GROUP), GROUP)
        return pltpu.make_async_copy(
            tr_hbm.at[:, :, rows, :], trs.at[:, :, rows, :], tr_sem.at[g]
        )

    for g in range(NGROUPS):
        group_copy(g).start()
    c_u = pltpu.make_async_copy(u_hbm, us, uv_sem.at[0])
    c_v = pltpu.make_async_copy(v_hbm, vs, uv_sem.at[1])

    for ref in (mx, lx, xa, ya, xb, yb):
        for t in range(3):
            ref[t, pl.ds(0, HALO), :] = jnp.zeros((HALO, LANES), F32)
            ref[t, pl.ds(EXT - HALO, HALO), :] = jnp.zeros((HALO, LANES), F32)

    pack[pl.ds(ROWS, 2 * LANES - ROWS), :] = jnp.zeros((2 * LANES - ROWS, LANES), F32)

    for c in c_mask + c_lev:
        c.wait()
    for t in range(2):
        depth = (lev_s[t] * mask_s[t]).astype(F32)
        lx[t, pl.ds(FIRST, ROWS), :] = depth
        own_ref[2, t] = depth
        mx[t, pl.ds(FIRST, ROWS), :] = jnp.where(depth > 0.0, 1.0, 0.0)
        turned = jnp.transpose(depth)
        if t == 0:
            l_s[...] = turned[:HALO]
        else:
            l_n[...] = turned[LANES - HALO :]
    for c in c_tx + c_ty + c_e0:
        c.wait()
    for t in range(2):
        wet = lx[t, pl.ds(FIRST, ROWS), :] > 0.0
        for i in range(2):
            value = jnp.where(wet, raw_s[i, t], 0.0)
            own_ref[i, t] = value
            fx[1 + i, t, pl.ds(FIRST, ROWS), :] = value

    def turn_edges(f):
        f_s[f] = jnp.transpose(fx[f, 0, pl.ds(FIRST, ROWS), :])[:HALO]
        f_n[f] = jnp.transpose(fx[f, 1, pl.ds(FIRST, ROWS), :])[LANES - HALO :]

    for f in range(3):
        turn_edges(f)

    glanes = lane_ids(GROUP)

    def force_group(g, carry):
        group_copy(g).wait()
        r0 = pl.multiple_of(g * GROUP, GROUP)
        depth = [lx[t, pl.ds(r0 + FIRST, GROUP), :] for t in range(2)]
        total = [jnp.zeros((GROUP, LANES), F32) for _ in range(2)]
        cols = jnp.zeros((GROUP, LANES), F32)
        for k in range(LEVELS):
            kept = {}
            for t in range(2):
                lanes = pl.ds(t * LANES, LANES)
                left = depth[t] - float(k)
                wet = left > 0.0
                t0 = trs[0, k, pl.ds(r0, GROUP), lanes]
                t1 = trs[1, k, pl.ds(r0, GROUP), lanes]
                total[t] = total[t] + jnp.maximum(left, 0.0) * (0.8 * t0 - 0.6 * t1)
                for i, value in enumerate((t0, t1)):
                    plane = i * LEVELS + k
                    value = jnp.where(wet, value, 0.0)
                    psc[plane, t, pl.ds(r0 + HALO, GROUP), :] = value
                    kept[t, i] = value
            for i in range(2):
                lane = 2 * (i * LEVELS + k)
                moved = pltpu.roll(jnp.where(glanes == 0, kept[0, i], kept[1, i]), lane + 1, 1)
                cols = jnp.where((glanes >= lane) & (glanes <= lane + 1), moved, cols)
        pack[pl.ds(r0, GROUP), :] = cols
        for t in range(2):
            rows = pl.ds(r0 + FIRST, GROUP)
            fx[3, t, rows, :] = total[t] * (1.0 / LEVELS) + 0.5 * fx[0, t, rows, :]
        return carry

    lax.fori_loop(0, EARLY_GROUPS, force_group, 0)

    pl.semaphore_wait(barrier, len(greeted))

    started = [0]

    def remote(src, dst, who):
        slot = started[0]
        started[0] += 1
        copy = pltpu.make_async_remote_copy(
            src_ref=src,
            dst_ref=dst,
            send_sem=send_sem.at[slot],
            recv_sem=recv_sem.at[slot],
            device_id=who,
            device_id_type=MESH,
        )
        copy.start()
        return copy

    high, low = pl.ds(LAST - HALO, HALO), pl.ds(FIRST, HALO)
    below, above = pl.ds(FIRST - HALO, HALO), pl.ds(LAST, HALO)
    both = pl.ds(0, 2)
    depth_copies = [
        remote(lx.at[1, high, :], l_co.at[0], (east, north)),
        remote(lx.at[0, high, :], l_co.at[1], (east, south)),
        remote(lx.at[1, low, :], l_co.at[2], (west, north)),
        remote(lx.at[0, low, :], l_co.at[3], (west, south)),
        remote(lx.at[both, high, :], lx.at[both, below, :], (east, gy)),
        remote(lx.at[both, low, :], lx.at[both, above, :], (west, gy)),
        remote(l_n, l_th.at[pl.ds(LANES - HALO, HALO), :], (gx, north)),
        remote(l_s, l_th.at[pl.ds(0, HALO), :], (gx, south)),
    ]

    def send_fields(which):
        return [
            remote(fx.at[which, both, high, :], fx.at[which, both, below, :], (east, gy)),
            remote(fx.at[which, both, low, :], fx.at[which, both, above, :], (west, gy)),
            remote(f_n.at[which], f_th.at[which, pl.ds(LANES - HALO, HALO), :], (gx, north)),
            remote(f_s.at[which], f_th.at[which, pl.ds(0, HALO), :], (gx, south)),
            remote(fx.at[which, 1, high, :], f_co.at[0, which], (east, north)),
            remote(fx.at[which, 0, high, :], f_co.at[1, which], (east, south)),
            remote(fx.at[which, 1, low, :], f_co.at[2, which], (west, north)),
            remote(fx.at[which, 0, low, :], f_co.at[3, which], (west, south)),
        ]

    field_copies = send_fields(pl.ds(0, 3))

    lax.fori_loop(EARLY_GROUPS, NGROUPS, force_group, 0)
    c_u.start()
    c_v.start()
    for plane in range(2 * LEVELS):
        for t in range(2):
            row_w[pl.ds(2 * plane + t, 1), :] = psc[plane, t, pl.ds(HALO, 1), :]
            row_e[pl.ds(2 * plane + t, 1), :] = psc[plane, t, pl.ds(HALO + ROWS - 1, 1), :]
    planes = 2 * LEVELS
    for h in range(2):
        turned_p[h] = jnp.transpose(pack[pl.ds(h * LANES, LANES), :])
        col_n[h] = turned_p[h, pl.ds(0, planes, stride=2), :]
        col_s[h] = turned_p[h, pl.ds(1, planes, stride=2), :]
    tracer_copies = [
        remote(row_e, got_w, (east, gy)),
        remote(row_w, got_e, (west, gy)),
        remote(col_n, got_s, (gx, north)),
        remote(col_s, got_n, (gx, south)),
    ]
    turn_edges(3)
    force_copies = send_fields(pl.ds(3, 1))

    lanes8 = lane_ids(HALO)
    lanes_all = lane_ids(ROWS)

    def inside(lanes):
        return ((lanes < HALO) & (gy < ny - 1)) | ((lanes >= LANES - HALO) & (gy > 0))

    def third_tile(dst, turned, co):
        keep8 = inside(lanes8)
        dst[2, pl.ds(FIRST, ROWS), :] = jnp.where(inside(lanes_all), jnp.transpose(turned), 0.0)
        dst[2, below, :] = jnp.where(keep8, jnp.where(lanes8 < HALO, co[1], co[0]), 0.0)
        dst[2, above, :] = jnp.where(keep8, jnp.where(lanes8 < HALO, co[3], co[2]), 0.0)

    for c in depth_copies:
        c.wait_recv()
    third_tile(lx, l_th[...], [l_co[i] for i in range(4)])

    n_tiles = (EXT - 2 * HALO) // HALO
    for i in range(n_tiles):
        rows = pl.ds(HALO + i * HALO, HALO)
        for t in range(3):
            if t == 2 or i == 0 or i == n_tiles - 1:
                mx[t, rows, :] = jnp.where(lx[t, rows, :] > 0.0, 1.0, 0.0)

    lanes16 = lane_ids(CHUNK)

    def diagonal(r0, size, lanes):
        rows = pl.ds(r0, size)
        sum_m = nine_sum(mx, r0, size, lanes)
        sum_l = nine_sum(lx, r0, size, lanes)
        values = []
        for t in range(3):
            value = 0.5 + 0.125 * (lx[t, rows, :] * sum_m[t] + mx[t, rows, :] * sum_l[t])
            inv[t, rows, :] = value
            values.append(value)
        return values

    def diagonal_rows(i, largest):
        values = diagonal(FIRST + i * CHUNK, CHUNK, lanes16)
        return jnp.maximum(largest, jnp.maximum(values[0], values[1]))

    largest = jnp.zeros((CHUNK, LANES), F32)
    for i in range(NCHUNKS):
        largest = diagonal_rows(i, largest)
    mine[...] = jnp.maximum(largest[:HALO], largest[HALO:])

    across = [remote(mine, max_x.at[d], plane_mates[d]) for d in plane_order]

    def each_row(body):
        for i in range((EXT - 2 * HALO) // CHUNK):
            body(HALO + i * CHUNK)

    diagonal(FIRST - HALO, HALO, lanes8)
    diagonal(LAST, HALO, lanes8)
    keep16 = inside(lanes16)

    def weights(r0):
        rows = pl.ds(r0, CHUNK)
        for t in range(3):
            recip = 1.0 / inv[t, rows, :]
            if t == 2:
                recip = jnp.where(keep16, recip, 0.0)
            inv[t, rows, :] = recip
            eighth = 0.125 * recip
            a1[t, rows, :] = eighth * lx[t, rows, :]
            a2[t, rows, :] = eighth * mx[t, rows, :]

    each_row(weights)

    for c in field_copies:
        c.wait_recv()
    for f in range(3):
        third_tile(fx.at[f], f_th[f], [f_co[i, f] for i in range(4)])

    def split_start(r0):
        rows = pl.ds(r0, CHUNK)
        for t in range(3):
            value = fx[0, t, rows, :]
            ext_ref[0, t, rows, :] = value
            xa[t, rows, :] = mx[t, rows, :] * value
            ya[t, rows, :] = lx[t, rows, :] * value

    each_row(split_start)

    def apply(x_ref, y_ref, r0):
        rows = pl.ds(r0, CHUNK)
        sum_x = nine_sum(x_ref, r0, CHUNK, lanes16)
        sum_y = nine_sum(y_ref, r0, CHUNK, lanes16)
        return [a1[t, rows, :] * sum_x[t] + a2[t, rows, :] * sum_y[t] for t in range(3)]

    def first_part(r0):
        rows = pl.ds(r0, CHUNK)
        moved = apply(xa, ya, r0)
        flux = [fx[2, t, rows, :] for t in range(3)]
        flux_n, flux_s = to_north(flux, lanes16), to_south(flux, lanes16)
        for t in range(3):
            div = fx[1, t, pl.ds(r0 + 1, CHUNK), :] - fx[1, t, pl.ds(r0 - 1, CHUNK), :]
            div = div + (flux_n[t] - flux_s[t])
            zx[t, rows, :] = (moved[t] - fx[0, t, rows, :]) - 0.25 * inv[t, rows, :] * div

    each_row(first_part)

    def marks(depth, base):
        count = jnp.clip(depth.astype(I32) - base, 0, 8)
        return jnp.left_shift(jnp.ones_like(count), 3 * count) - 1

    each = 0o11111111
    def count_wet(i):
        r0 = FIRST + i * CHUNK
        rows = pl.ds(r0, CHUNK)
        for half in range(2):
            base = 8 * half
            here = [marks(lx[t, rows, :], base) for t in range(3)]
            bits = [h & each for h in here]
            n_bits, s_bits = to_north(bits, lanes16), to_south(bits, lanes16)
            for t in range(2):
                e_bits = marks(lx[t, pl.ds(r0 + 1, CHUNK), :], base) & each
                w_bits = marks(lx[t, pl.ds(r0 - 1, CHUNK), :], base) & each
                total = (n_bits[t] + s_bits[t]) + (e_bits + w_bits)
                cnt[half, t, pl.ds(i * CHUNK, CHUNK), :] = total & here[t]

    for i in range(NCHUNKS):
        count_wet(i)

    for c in force_copies:
        c.wait_recv()
    third_tile(fx.at[3], f_th[3], [f_co[i, 3] for i in range(4)])

    def add_force(r0):
        rows = pl.ds(r0, CHUNK)
        for t in range(3):
            value = zx[t, rows, :] + inv[t, rows, :] * fx[3, t, rows, :]
            zx[t, rows, :] = value
            xb[t, rows, :] = mx[t, rows, :] * value
            yb[t, rows, :] = lx[t, rows, :] * value

    def first_power(r0):
        rows = pl.ds(r0, CHUNK)
        moved = apply(xb, yb, r0)
        for t in range(3):
            value = zx[t, rows, :] + moved[t]
            ext_ref[1, t, rows, :] = value
            xa[t, rows, :] = mx[t, rows, :] * value
            ya[t, rows, :] = lx[t, rows, :] * value

    def second_power(r0):
        rows = pl.ds(r0, CHUNK)
        moved = apply(xa, ya, r0)
        for t in range(3):
            xb[t, rows, :] = moved[t]
            yb[t, rows, :] = lx[t, rows, :] * moved[t]

    def third_power(r0):
        rows = pl.ds(r0, CHUNK)
        moved = apply(xb, yb, r0)
        for t in range(3):
            ext_ref[2, t, rows, :] = moved[t]

    for body in (add_force, first_power, second_power, third_power):
        each_row(body)

    for c in tracer_copies:
        c.wait_recv()
    for plane in range(2 * LEVELS):
        for t in range(2):
            psc[plane, t, pl.ds(HALO - 1, 1), :] = got_w[pl.ds(2 * plane + t, 1), :]
            psc[plane, t, pl.ds(HALO + ROWS, 1), :] = got_e[pl.ds(2 * plane + t, 1), :]
    for h in range(2):
        turned_p[h, pl.ds(0, planes, stride=2), :] = jnp.where(gy < ny - 1, got_n[h], 0.0)
        turned_p[h, pl.ds(1, planes, stride=2), :] = jnp.where(gy > 0, got_s[h], 0.0)
        edge[pl.ds(h * LANES, LANES), :] = jnp.transpose(turned_p[h])
    c_u.wait()
    c_v.wait()

    def step_chunk(i, carry):
        row = pl.multiple_of(i * CHUNK, CHUNK)
        tracer_chunk(i, trs, us, vs, psc, own_ref, cnt, edge, out_ref, row)
        return carry

    lax.fori_loop(0, FIRST_CHUNKS, step_chunk, 0)

    for c in across:
        c.wait_recv()
    largest = mine[...]
    for d in range(len(across)):
        largest = jnp.maximum(largest, max_x[d])
    mid[...] = largest
    along = [remote(mid, max_y.at[d], mate) for d, mate in enumerate(line_mates)]

    lax.fori_loop(FIRST_CHUNKS, STEP_CHUNKS, step_chunk, 0)

    for c in along:
        c.wait_recv()
    for d in range(len(along)):
        largest = jnp.maximum(largest, max_y[d])
    peak_ref[...] = largest
    for c in depth_copies + field_copies + tracer_copies + force_copies + across + along:
        c.wait_send()


def finish_kernel(
    big, ext, own, peak, trs, us, vs, psc, cnt, edge,
    tr_out, surf_out, tx_out, ty_out,
    sx, stage, late, sem, late_sem, out_sem,
):
    copies = []
    done = pl.ds(0, STEP_CHUNKS * CHUNK)
    for c in range(2):
        for q in range(4):
            levels = pl.ds(4 * q, 4)
            copies.append(
                pltpu.make_async_copy(
                    big.at[c, levels], tr_out.at[c, levels, done, :], sem.at[4 * c + q]
                )
            )
    for c in copies:
        c.start()

    def late_copy(i):
        row = pl.multiple_of(i * CHUNK, CHUNK)
        left = pl.multiple_of(row - STEP_CHUNKS * CHUNK, CHUNK)
        return pltpu.make_async_copy(
            late.at[:, :, pl.ds(left, CHUNK), :],
            tr_out.at[:, :, pl.ds(row, CHUNK), :],
            late_sem.at[i - STEP_CHUNKS],
        )

    def late_chunk(i, carry):
        left = pl.multiple_of((i - STEP_CHUNKS) * CHUNK, CHUNK)
        tracer_chunk(i, trs, us, vs, psc, own, cnt, edge, late, left)
        late_copy(i).start()
        return carry

    lax.fori_loop(STEP_CHUNKS, NCHUNKS, late_chunk, 0)
    top = jnp.zeros((HALO, LANES), F32) + jnp.max(peak[...], axis=(0, 1), keepdims=True)
    lowest = 0.5 / top
    scale = 1.0 / (1.0 - lowest)
    four = 4.0 * scale * scale
    w2 = 1.0 / (1.0 - 2.0 / four)
    w3 = 1.0 / (1.0 - w2 / four)
    w4 = 1.0 / (1.0 - w3 / four)
    c0 = 1.0 - (w2 - 1.0) * (w4 - 1.0)
    c2 = w2 * w3 * w4
    for i in range((EXT - 2 * HALO) // HALO):
        rows = pl.ds(HALO + i * HALO, HALO)
        for t in range(3):
            sx[t, rows, :] = ext[0, t, rows, :] + (c0 * ext[1, t, rows, :] + c2 * ext[2, t, rows, :])
    lanes8 = lane_ids(HALO)
    for i in range(ROWS // HALO):
        r0 = FIRST + i * HALO
        rows, dst = pl.ds(r0, HALO), pl.ds(i * HALO, HALO)
        surf = [sx[t, rows, :] for t in range(3)]
        n_val, s_val = to_north(surf, lanes8), to_south(surf, lanes8)
        for t in range(2):
            lanes = pl.ds(t * LANES, LANES)
            wet = jnp.where(own[2, t, dst, :] > 0.0, 0.25, 0.0)
            diff = sx[t, pl.ds(r0 + 1, HALO), :] - sx[t, pl.ds(r0 - 1, HALO), :]
            stage[0, dst, lanes] = surf[t]
            stage[1, dst, lanes] = own[0, t, dst, :] - wet * diff
            stage[2, dst, lanes] = own[1, t, dst, :] - wet * (n_val[t] - s_val[t])
    ends = []
    for i, ref in enumerate((surf_out, tx_out, ty_out)):
        ends.append(pltpu.make_async_copy(stage.at[i], ref, out_sem.at[i]))
    for c in ends:
        c.start()
    for c in copies + ends:
        c.wait()
    for i in range(STEP_CHUNKS, NCHUNKS):
        late_copy(i).wait()


def in_hbm(value):
    return pltpu.with_memory_space_constraint(value, pltpu.HBM)


def local(tracer, zonal, merid, surface, flow_x, flow_y, land_mask, levels):
    hbm = pl.BlockSpec(memory_space=pltpu.HBM)
    vmem = pl.BlockSpec(memory_space=pltpu.VMEM)
    wide = pltpu.VMEM((3, EXT, LANES), F32)
    n_remote = 28 + 15 + 7
    planes = 2 * LEVELS
    left = ROWS - STEP_CHUNKS * CHUNK
    args = (tracer, zonal, merid, surface, flow_x, flow_y, land_mask, levels)
    kept = pl.pallas_call(
        step_kernel,
        out_shape=(
            pltpu.VMEM((2, LEVELS, STEP_CHUNKS * CHUNK, COLS), F32),
            pltpu.VMEM((3, 3, EXT, LANES), F32),
            pltpu.VMEM((3, 2, ROWS, LANES), F32),
            pltpu.VMEM((HALO, LANES), F32),
            pltpu.VMEM((2, LEVELS, ROWS, COLS), F32),
            pltpu.VMEM((LEVELS, ROWS, COLS), jnp.bfloat16),
            pltpu.VMEM((LEVELS, ROWS, COLS), jnp.bfloat16),
            pltpu.VMEM((planes, 2, ROWS + 2 * HALO, LANES), F32),
            pltpu.VMEM((2, 2, ROWS, LANES), I32),
            pltpu.VMEM((2 * LANES, LANES), F32),
        ),
        in_specs=[hbm] * 8,
        out_specs=(vmem,) * 10,
        scratch_shapes=[
            pltpu.VMEM((2, ROWS, LANES), I32),
            pltpu.VMEM((2, ROWS, LANES), I32),
            pltpu.VMEM((2, 2, ROWS, LANES), F32),
            wide,
            pltpu.VMEM((4, 3, EXT, LANES), F32),
            wide, wide, wide, wide, wide, wide, wide, wide, wide,
            pltpu.VMEM((2 * planes, LANES), F32),
            pltpu.VMEM((2 * planes, LANES), F32),
            pltpu.VMEM((2 * planes, LANES), F32),
            pltpu.VMEM((2 * planes, LANES), F32),
            pltpu.VMEM((2 * LANES, LANES), F32),
            pltpu.VMEM((2, LANES, LANES), F32),
            pltpu.VMEM((2, planes, LANES), F32),
            pltpu.VMEM((2, planes, LANES), F32),
            pltpu.VMEM((2, planes, LANES), F32),
            pltpu.VMEM((2, planes, LANES), F32),
            pltpu.VMEM((HALO, ROWS), F32),
            pltpu.VMEM((HALO, ROWS), F32),
            pltpu.VMEM((LANES, ROWS), F32),
            pltpu.VMEM((4, HALO, LANES), F32),
            pltpu.VMEM((4, HALO, ROWS), F32),
            pltpu.VMEM((4, HALO, ROWS), F32),
            pltpu.VMEM((4, LANES, ROWS), F32),
            pltpu.VMEM((4, 4, HALO, LANES), F32),
            pltpu.VMEM((HALO, LANES), F32),
            pltpu.VMEM((HALO, LANES), F32),
            pltpu.VMEM((15, HALO, LANES), F32),
            pltpu.VMEM((7, HALO, LANES), F32),
            pltpu.SemaphoreType.DMA((10,)),
            pltpu.SemaphoreType.DMA((NGROUPS,)),
            pltpu.SemaphoreType.DMA((2,)),
            pltpu.SemaphoreType.DMA((n_remote,)),
            pltpu.SemaphoreType.DMA((n_remote,)),
        ],
        compiler_params=pltpu.CompilerParams(
            collective_id=1, has_side_effects=True, vmem_limit_bytes=20 << 20
        ),
        name="ocean_step",
    )(*[in_hbm(a) for a in args])
    return pl.pallas_call(
        finish_kernel,
        out_shape=(
            jax.ShapeDtypeStruct((2, LEVELS, ROWS, COLS), F32),
            jax.ShapeDtypeStruct((ROWS, COLS), F32),
            jax.ShapeDtypeStruct((ROWS, COLS), F32),
            jax.ShapeDtypeStruct((ROWS, COLS), F32),
        ),
        in_specs=[vmem] * 10,
        out_specs=(hbm,) * 4,
        scratch_shapes=[
            wide,
            pltpu.VMEM((3, ROWS, COLS), F32),
            pltpu.VMEM((2, LEVELS, left, COLS), F32),
            pltpu.SemaphoreType.DMA((8,)),
            pltpu.SemaphoreType.DMA((left // CHUNK,)),
            pltpu.SemaphoreType.DMA((3,)),
        ],
        compiler_params=pltpu.CompilerParams(vmem_limit_bytes=20 << 20),
        name="ocean_finish",
    )(*kept)


def solution(mesh):
    flat = P("gx", "gy")
    deep = P(None, "gx", "gy")
    full = P(None, None, "gx", "gy")
    return jax.shard_map(
        local,
        mesh=mesh,
        in_specs=(full, deep, deep, flat, flat, flat, flat, flat),
        out_specs=(full, flat, flat, flat),
        check_vma=False,
    )
```

```python
import jax
import jax.numpy as jnp
from jax import lax
from jax.experimental import pallas as pl
from jax.experimental.pallas import tpu as pltpu
from jax.sharding import PartitionSpec as P

MESH = pl.DeviceIdType.MESH
F32 = jnp.float32
I32 = jnp.int32

LEVELS = 16
ROWS = 224
COLS = 256
LANES = 128
HALO = 8
FIRST = 16
LAST = FIRST + ROWS
EXT = 256
GROUP = 32
NGROUPS = ROWS // GROUP
CHUNK = 16
NCHUNKS = ROWS // CHUNK
FIRST_CHUNKS = 2
STEP_CHUNKS = 11


def lane_ids(rows):
    return lax.broadcasted_iota(I32, (rows, LANES), 1)


def to_north(tiles, lanes):
    moved = [pltpu.roll(t, LANES - 1, 1) for t in tiles]
    n = len(tiles)
    return [jnp.where(lanes == LANES - 1, moved[(i + 1) % n], moved[i]) for i in range(n)]


def to_south(tiles, lanes):
    moved = [pltpu.roll(t, 1, 1) for t in tiles]
    n = len(tiles)
    return [jnp.where(lanes == 0, moved[(i - 1) % n], moved[i]) for i in range(n)]


def nine_sum(ref, r0, rows, lanes):
    sides, inner = [], []
    for t in range(3):
        here = ref[t, pl.ds(r0, rows), :]
        pair = ref[t, pl.ds(r0 + 1, rows), :] + ref[t, pl.ds(r0 - 1, rows), :]
        sides.append(pair)
        inner.append(here + 0.5 * pair)
    north = to_north(inner, lanes)
    south = to_south(inner, lanes)
    return [sides[t] + (north[t] + south[t]) for t in range(3)]


def tracer_chunk(i, trs, us, vs, psc, own, cnt, edge, out, out_row):
    lanes16 = lane_ids(CHUNK)
    top, bottom = lanes16 == LANES - 1, lanes16 == 0
    r0 = pl.multiple_of(i * CHUNK, CHUNK)
    rows = pl.ds(r0, CHUNK)
    halo = r0 + HALO
    beside = edge[rows, :]
    depth = [own[2, t, rows, :] for t in range(2)]
    for k in range(LEVELS):
        half, shift = k // 8, 3 * (k % 8)
        coef = []
        for t in range(2):
            lanes = pl.ds(t * LANES, LANES)
            wet = depth[t] > float(k)
            fifth = jnp.where(wet, 0.2, 0.0)
            quarter = jnp.where(wet, 0.25, 0.0)
            fast_x = us[k, rows, lanes].astype(F32) * quarter
            fast_y = vs[k, rows, lanes].astype(F32) * quarter
            number = jnp.right_shift(cnt[half, t, rows, :], shift) & 7
            centre = 1.0 - 0.2 * number.astype(F32)
            coef.append((centre, fifth - fast_x, fifth + fast_x, fifth - fast_y, fifth + fast_y))
        for c in range(2):
            plane = c * LEVELS + k
            here = [psc[plane, t, pl.ds(halo, CHUNK), :] for t in range(2)]
            ends = pltpu.roll(beside, LANES - 1 - 2 * plane, 1)
            up = [pltpu.roll(p, LANES - 1, 1) for p in here]
            down = [pltpu.roll(p, 1, 1) for p in here]
            north_p = [jnp.where(top, up[1], up[0]), jnp.where(top, ends, up[1])]
            south_p = [jnp.where(bottom, ends, down[0]), jnp.where(bottom, down[0], down[1])]
            for t in range(2):
                lanes = pl.ds(t * LANES, LANES)
                centre, k_e, k_w, k_n, k_s = coef[t]
                value = centre * trs[c, k, rows, lanes]
                value = value + k_e * psc[plane, t, pl.ds(halo + 1, CHUNK), :]
                value = value + k_w * psc[plane, t, pl.ds(halo - 1, CHUNK), :]
                out[c, k, pl.ds(out_row, CHUNK), lanes] = value + (
                    k_n * north_p[t] + k_s * south_p[t]
                )


def step_kernel(
    tr_hbm, u_hbm, v_hbm, e0_hbm, tx_hbm, ty_hbm, mask_hbm, lev_hbm,
    out_ref, ext_ref, own_ref, peak_ref, trs, us, vs, psc, cnt, edge,
    mask_s, lev_s, raw_s,
    lx, fx, mx, a1, a2, inv, xa, ya, xb, yb, zx,
    row_e, row_w, got_e, got_w, pack, turned_p, col_n, col_s, got_n, got_s,
    l_n, l_s, l_th, l_co, f_n, f_s, f_th, f_co,
    mine, mid, max_x, max_y,
    in_sem, tr_sem, uv_sem, send_sem, recv_sem,
):
    gx = lax.axis_index("gx")
    gy = lax.axis_index("gy")
    nx, ny = 16, 8
    east, west = lax.rem(gx + 1, nx), lax.rem(gx + nx - 1, nx)
    north, south = lax.rem(gy + 1, ny), lax.rem(gy + ny - 1, ny)
    corners = ((east, north), (east, south), (west, north), (west, south))
    ring, x_hi, core = gx // 4, lax.rem(gx // 2, 2), lax.rem(gx, 2)
    plane_mates = [
        (ring * 4 + lax.rem(x_hi + d // 8, 2) * 2 + core, lax.rem(gy + d % 8, ny))
        for d in range(1, 16)
    ]
    line_mates = [
        (lax.rem(ring + d % 4, 4) * 4 + x_hi * 2 + lax.rem(core + d // 4, 2), gy)
        for d in range(1, 8)
    ]
    sides = ((east, gy), (west, gy))

    barrier = pltpu.get_barrier_semaphore()
    plane_order = (9, 13, 8, 10, 12, 14, 7, 11, 1, 5, 0, 2, 4, 6, 3)
    greeted = (*corners, *sides, *[plane_mates[d] for d in plane_order], *line_mates)
    for mate in greeted:
        pl.semaphore_signal(barrier, inc=1, device_id=mate, device_id_type=MESH)

    def flat_copy(src, dst, slot):
        copies = []
        for t in range(2):
            copies.append(
                pltpu.make_async_copy(
                    src.at[:, pl.ds(t * LANES, LANES)], dst(t), in_sem.at[2 * slot + t]
                )
            )
        for c in copies:
            c.start()
        return copies

    c_mask = flat_copy(mask_hbm, lambda t: mask_s.at[t], 0)
    c_lev = flat_copy(lev_hbm, lambda t: lev_s.at[t], 1)
    c_tx = flat_copy(tx_hbm, lambda t: raw_s.at[0, t], 2)
    c_ty = flat_copy(ty_hbm, lambda t: raw_s.at[1, t], 3)
    c_e0 = flat_copy(e0_hbm, lambda t: fx.at[0, t, pl.ds(FIRST, ROWS), :], 4)

    def group_copy(g):
        rows = pl.ds(pl.multiple_of(g * GROUP, GROUP), GROUP)
        return pltpu.make_async_copy(
            tr_hbm.at[:, :, rows, :], trs.at[:, :, rows, :], tr_sem.at[g]
        )

    for g in range(NGROUPS):
        group_copy(g).start()
    c_u = pltpu.make_async_copy(u_hbm, us, uv_sem.at[0])
    c_v = pltpu.make_async_copy(v_hbm, vs, uv_sem.at[1])

    for ref in (mx, lx, xa, ya, xb, yb):
        for t in range(3):
            ref[t, pl.ds(0, HALO), :] = jnp.zeros((HALO, LANES), F32)
            ref[t, pl.ds(EXT - HALO, HALO), :] = jnp.zeros((HALO, LANES), F32)

    pack[pl.ds(ROWS, 2 * LANES - ROWS), :] = jnp.zeros((2 * LANES - ROWS, LANES), F32)

    for c in c_mask + c_lev:
        c.wait()
    for t in range(2):
        depth = (lev_s[t] * mask_s[t]).astype(F32)
        lx[t, pl.ds(FIRST, ROWS), :] = depth
        turned = jnp.transpose(depth)
        if t == 0:
            l_s[...] = turned[:HALO]
        else:
            l_n[...] = turned[LANES - HALO :]

    pl.semaphore_wait(barrier, len(greeted))

    started = [0]

    def remote(src, dst, who):
        slot = started[0]
        started[0] += 1
        copy = pltpu.make_async_remote_copy(
            src_ref=src,
            dst_ref=dst,
            send_sem=send_sem.at[slot],
            recv_sem=recv_sem.at[slot],
            device_id=who,
            device_id_type=MESH,
        )
        copy.start()
        return copy

    high, low = pl.ds(LAST - HALO, HALO), pl.ds(FIRST, HALO)
    below, above = pl.ds(FIRST - HALO, HALO), pl.ds(LAST, HALO)
    both = pl.ds(0, 2)
    depth_copies = [
        remote(lx.at[1, high, :], l_co.at[0], (east, north)),
        remote(lx.at[0, high, :], l_co.at[1], (east, south)),
        remote(lx.at[1, low, :], l_co.at[2], (west, north)),
        remote(lx.at[0, low, :], l_co.at[3], (west, south)),
        remote(lx.at[both, high, :], lx.at[both, below, :], (east, gy)),
        remote(lx.at[both, low, :], lx.at[both, above, :], (west, gy)),
        remote(l_n, l_th.at[pl.ds(LANES - HALO, HALO), :], (gx, north)),
        remote(l_s, l_th.at[pl.ds(0, HALO), :], (gx, south)),
    ]

    for c in c_tx + c_ty + c_e0:
        c.wait()
    for t in range(2):
        depth = lx[t, pl.ds(FIRST, ROWS), :]
        own_ref[2, t] = depth
        wet = depth > 0.0
        mx[t, pl.ds(FIRST, ROWS), :] = jnp.where(wet, 1.0, 0.0)
        for i in range(2):
            value = jnp.where(wet, raw_s[i, t], 0.0)
            own_ref[i, t] = value
            fx[1 + i, t, pl.ds(FIRST, ROWS), :] = value

    def turn_edges(f):
        f_s[f] = jnp.transpose(fx[f, 0, pl.ds(FIRST, ROWS), :])[:HALO]
        f_n[f] = jnp.transpose(fx[f, 1, pl.ds(FIRST, ROWS), :])[LANES - HALO :]

    for f in range(3):
        turn_edges(f)

    def send_fields(which):
        return [
            remote(fx.at[which, both, high, :], fx.at[which, both, below, :], (east, gy)),
            remote(fx.at[which, both, low, :], fx.at[which, both, above, :], (west, gy)),
            remote(f_n.at[which], f_th.at[which, pl.ds(LANES - HALO, HALO), :], (gx, north)),
            remote(f_s.at[which], f_th.at[which, pl.ds(0, HALO), :], (gx, south)),
            remote(fx.at[which, 1, high, :], f_co.at[0, which], (east, north)),
            remote(fx.at[which, 0, high, :], f_co.at[1, which], (east, south)),
            remote(fx.at[which, 1, low, :], f_co.at[2, which], (west, north)),
            remote(fx.at[which, 0, low, :], f_co.at[3, which], (west, south)),
        ]

    field_copies = send_fields(pl.ds(0, 3))

    glanes = lane_ids(GROUP)

    def force_group(g, carry):
        group_copy(g).wait()
        r0 = pl.multiple_of(g * GROUP, GROUP)
        depth = [lx[t, pl.ds(r0 + FIRST, GROUP), :] for t in range(2)]
        total = [jnp.zeros((GROUP, LANES), F32) for _ in range(2)]
        cols = jnp.zeros((GROUP, LANES), F32)
        for k in range(LEVELS):
            kept = {}
            for t in range(2):
                lanes = pl.ds(t * LANES, LANES)
                left = depth[t] - float(k)
                wet = left > 0.0
                t0 = trs[0, k, pl.ds(r0, GROUP), lanes]
                t1 = trs[1, k, pl.ds(r0, GROUP), lanes]
                total[t] = total[t] + jnp.maximum(left, 0.0) * (0.8 * t0 - 0.6 * t1)
                for i, value in enumerate((t0, t1)):
                    plane = i * LEVELS + k
                    value = jnp.where(wet, value, 0.0)
                    psc[plane, t, pl.ds(r0 + HALO, GROUP), :] = value
                    kept[t, i] = value
            for i in range(2):
                lane = 2 * (i * LEVELS + k)
                moved = pltpu.roll(jnp.where(glanes == 0, kept[0, i], kept[1, i]), lane + 1, 1)
                cols = jnp.where((glanes >= lane) & (glanes <= lane + 1), moved, cols)
        pack[pl.ds(r0, GROUP), :] = cols
        for t in range(2):
            rows = pl.ds(r0 + FIRST, GROUP)
            fx[3, t, rows, :] = total[t] * (1.0 / LEVELS) + 0.5 * fx[0, t, rows, :]
        return carry

    lax.fori_loop(0, NGROUPS, force_group, 0)
    c_u.start()
    c_v.start()
    for plane in range(2 * LEVELS):
        for t in range(2):
            row_w[pl.ds(2 * plane + t, 1), :] = psc[plane, t, pl.ds(HALO, 1), :]
            row_e[pl.ds(2 * plane + t, 1), :] = psc[plane, t, pl.ds(HALO + ROWS - 1, 1), :]
    planes = 2 * LEVELS
    for h in range(2):
        turned_p[h] = jnp.transpose(pack[pl.ds(h * LANES, LANES), :])
        col_n[h] = turned_p[h, pl.ds(0, planes, stride=2), :]
        col_s[h] = turned_p[h, pl.ds(1, planes, stride=2), :]
    tracer_copies = [
        remote(row_e, got_w, (east, gy)),
        remote(row_w, got_e, (west, gy)),
        remote(col_n, got_s, (gx, north)),
        remote(col_s, got_n, (gx, south)),
    ]
    turn_edges(3)
    force_copies = send_fields(pl.ds(3, 1))

    lanes8 = lane_ids(HALO)
    lanes_all = lane_ids(ROWS)

    def inside(lanes):
        return ((lanes < HALO) & (gy < ny - 1)) | ((lanes >= LANES - HALO) & (gy > 0))

    def third_tile(dst, turned, co):
        keep8 = inside(lanes8)
        dst[2, pl.ds(FIRST, ROWS), :] = jnp.where(inside(lanes_all), jnp.transpose(turned), 0.0)
        dst[2, below, :] = jnp.where(keep8, jnp.where(lanes8 < HALO, co[1], co[0]), 0.0)
        dst[2, above, :] = jnp.where(keep8, jnp.where(lanes8 < HALO, co[3], co[2]), 0.0)

    for c in depth_copies:
        c.wait_recv()
    third_tile(lx, l_th[...], [l_co[i] for i in range(4)])

    n_tiles = (EXT - 2 * HALO) // HALO
    for i in range(n_tiles):
        rows = pl.ds(HALO + i * HALO, HALO)
        for t in range(3):
            if t == 2 or i == 0 or i == n_tiles - 1:
                mx[t, rows, :] = jnp.where(lx[t, rows, :] > 0.0, 1.0, 0.0)

    lanes16 = lane_ids(CHUNK)

    def diagonal(r0, size, lanes):
        rows = pl.ds(r0, size)
        sum_m = nine_sum(mx, r0, size, lanes)
        sum_l = nine_sum(lx, r0, size, lanes)
        values = []
        for t in range(3):
            value = 0.5 + 0.125 * (lx[t, rows, :] * sum_m[t] + mx[t, rows, :] * sum_l[t])
            inv[t, rows, :] = value
            values.append(value)
        return values

    def diagonal_rows(i, largest):
        values = diagonal(FIRST + i * CHUNK, CHUNK, lanes16)
        return jnp.maximum(largest, jnp.maximum(values[0], values[1]))

    largest = jnp.zeros((CHUNK, LANES), F32)
    for i in range(NCHUNKS):
        largest = diagonal_rows(i, largest)
    mine[...] = jnp.maximum(largest[:HALO], largest[HALO:])

    across = [remote(mine, max_x.at[d], plane_mates[d]) for d in plane_order]

    def each_row(body):
        for i in range((EXT - 2 * HALO) // CHUNK):
            body(HALO + i * CHUNK)

    diagonal(FIRST - HALO, HALO, lanes8)
    diagonal(LAST, HALO, lanes8)
    keep16 = inside(lanes16)

    def weights(r0):
        rows = pl.ds(r0, CHUNK)
        for t in range(3):
            recip = 1.0 / inv[t, rows, :]
            if t == 2:
                recip = jnp.where(keep16, recip, 0.0)
            inv[t, rows, :] = recip
            eighth = 0.125 * recip
            a1[t, rows, :] = eighth * lx[t, rows, :]
            a2[t, rows, :] = eighth * mx[t, rows, :]

    each_row(weights)

    for c in field_copies:
        c.wait_recv()
    for f in range(3):
        third_tile(fx.at[f], f_th[f], [f_co[i, f] for i in range(4)])

    def split_start(r0):
        rows = pl.ds(r0, CHUNK)
        for t in range(3):
            value = fx[0, t, rows, :]
            ext_ref[0, t, rows, :] = value
            xa[t, rows, :] = mx[t, rows, :] * value
            ya[t, rows, :] = lx[t, rows, :] * value

    each_row(split_start)

    def apply(x_ref, y_ref, r0):
        rows = pl.ds(r0, CHUNK)
        sum_x = nine_sum(x_ref, r0, CHUNK, lanes16)
        sum_y = nine_sum(y_ref, r0, CHUNK, lanes16)
        return [a1[t, rows, :] * sum_x[t] + a2[t, rows, :] * sum_y[t] for t in range(3)]

    def first_part(r0):
        rows = pl.ds(r0, CHUNK)
        moved = apply(xa, ya, r0)
        flux = [fx[2, t, rows, :] for t in range(3)]
        flux_n, flux_s = to_north(flux, lanes16), to_south(flux, lanes16)
        for t in range(3):
            div = fx[1, t, pl.ds(r0 + 1, CHUNK), :] - fx[1, t, pl.ds(r0 - 1, CHUNK), :]
            div = div + (flux_n[t] - flux_s[t])
            zx[t, rows, :] = (moved[t] - fx[0, t, rows, :]) - 0.25 * inv[t, rows, :] * div

    each_row(first_part)

    def marks(depth, base):
        count = jnp.clip(depth.astype(I32) - base, 0, 8)
        return jnp.left_shift(jnp.ones_like(count), 3 * count) - 1

    each = 0o11111111
    def count_wet(i):
        r0 = FIRST + i * CHUNK
        rows = pl.ds(r0, CHUNK)
        for half in range(2):
            base = 8 * half
            here = [marks(lx[t, rows, :], base) for t in range(3)]
            bits = [h & each for h in here]
            n_bits, s_bits = to_north(bits, lanes16), to_south(bits, lanes16)
            for t in range(2):
                e_bits = marks(lx[t, pl.ds(r0 + 1, CHUNK), :], base) & each
                w_bits = marks(lx[t, pl.ds(r0 - 1, CHUNK), :], base) & each
                total = (n_bits[t] + s_bits[t]) + (e_bits + w_bits)
                cnt[half, t, pl.ds(i * CHUNK, CHUNK), :] = total & here[t]

    for i in range(NCHUNKS):
        count_wet(i)

    for c in force_copies:
        c.wait_recv()
    third_tile(fx.at[3], f_th[3], [f_co[i, 3] for i in range(4)])

    def add_force(r0):
        rows = pl.ds(r0, CHUNK)
        for t in range(3):
            value = zx[t, rows, :] + inv[t, rows, :] * fx[3, t, rows, :]
            zx[t, rows, :] = value
            xb[t, rows, :] = mx[t, rows, :] * value
            yb[t, rows, :] = lx[t, rows, :] * value

    def first_power(r0):
        rows = pl.ds(r0, CHUNK)
        moved = apply(xb, yb, r0)
        for t in range(3):
            value = zx[t, rows, :] + moved[t]
            ext_ref[1, t, rows, :] = value
            xa[t, rows, :] = mx[t, rows, :] * value
            ya[t, rows, :] = lx[t, rows, :] * value

    def second_power(r0):
        rows = pl.ds(r0, CHUNK)
        moved = apply(xa, ya, r0)
        for t in range(3):
            xb[t, rows, :] = moved[t]
            yb[t, rows, :] = lx[t, rows, :] * moved[t]

    def third_power(r0):
        rows = pl.ds(r0, CHUNK)
        moved = apply(xb, yb, r0)
        for t in range(3):
            ext_ref[2, t, rows, :] = moved[t]

    for body in (add_force, first_power, second_power, third_power):
        each_row(body)

    for c in tracer_copies:
        c.wait_recv()
    for plane in range(2 * LEVELS):
        for t in range(2):
            psc[plane, t, pl.ds(HALO - 1, 1), :] = got_w[pl.ds(2 * plane + t, 1), :]
            psc[plane, t, pl.ds(HALO + ROWS, 1), :] = got_e[pl.ds(2 * plane + t, 1), :]
    for h in range(2):
        turned_p[h, pl.ds(0, planes, stride=2), :] = jnp.where(gy < ny - 1, got_n[h], 0.0)
        turned_p[h, pl.ds(1, planes, stride=2), :] = jnp.where(gy > 0, got_s[h], 0.0)
        edge[pl.ds(h * LANES, LANES), :] = jnp.transpose(turned_p[h])
    c_u.wait()
    c_v.wait()

    def step_chunk(i, carry):
        row = pl.multiple_of(i * CHUNK, CHUNK)
        tracer_chunk(i, trs, us, vs, psc, own_ref, cnt, edge, out_ref, row)
        return carry

    lax.fori_loop(0, FIRST_CHUNKS, step_chunk, 0)

    for c in across:
        c.wait_recv()
    largest = mine[...]
    for d in range(len(across)):
        largest = jnp.maximum(largest, max_x[d])
    mid[...] = largest
    along = [remote(mid, max_y.at[d], mate) for d, mate in enumerate(line_mates)]

    lax.fori_loop(FIRST_CHUNKS, STEP_CHUNKS, step_chunk, 0)

    for c in along:
        c.wait_recv()
    for d in range(len(along)):
        largest = jnp.maximum(largest, max_y[d])
    peak_ref[...] = largest
    for c in depth_copies + field_copies + tracer_copies + force_copies + across + along:
        c.wait_send()


def finish_kernel(
    big, ext, own, peak, trs, us, vs, psc, cnt, edge,
    tr_out, surf_out, tx_out, ty_out,
    sx, stage, late, sem, late_sem, out_sem,
):
    copies = []
    done = pl.ds(0, STEP_CHUNKS * CHUNK)
    for c in range(2):
        for q in range(4):
            levels = pl.ds(4 * q, 4)
            copies.append(
                pltpu.make_async_copy(
                    big.at[c, levels], tr_out.at[c, levels, done, :], sem.at[4 * c + q]
                )
            )
    for c in copies:
        c.start()

    def late_copy(i):
        row = pl.multiple_of(i * CHUNK, CHUNK)
        left = pl.multiple_of(row - STEP_CHUNKS * CHUNK, CHUNK)
        return pltpu.make_async_copy(
            late.at[:, :, pl.ds(left, CHUNK), :],
            tr_out.at[:, :, pl.ds(row, CHUNK), :],
            late_sem.at[i - STEP_CHUNKS],
        )

    def late_chunk(i, carry):
        left = pl.multiple_of((i - STEP_CHUNKS) * CHUNK, CHUNK)
        tracer_chunk(i, trs, us, vs, psc, own, cnt, edge, late, left)
        late_copy(i).start()
        return carry

    lax.fori_loop(STEP_CHUNKS, NCHUNKS, late_chunk, 0)
    top = jnp.zeros((HALO, LANES), F32) + jnp.max(peak[...], axis=(0, 1), keepdims=True)
    lowest = 0.5 / top
    scale = 1.0 / (1.0 - lowest)
    four = 4.0 * scale * scale
    w2 = 1.0 / (1.0 - 2.0 / four)
    w3 = 1.0 / (1.0 - w2 / four)
    w4 = 1.0 / (1.0 - w3 / four)
    c0 = 1.0 - (w2 - 1.0) * (w4 - 1.0)
    c2 = w2 * w3 * w4
    for i in range((EXT - 2 * HALO) // HALO):
        rows = pl.ds(HALO + i * HALO, HALO)
        for t in range(3):
            sx[t, rows, :] = ext[0, t, rows, :] + (c0 * ext[1, t, rows, :] + c2 * ext[2, t, rows, :])
    lanes8 = lane_ids(HALO)
    for i in range(ROWS // HALO):
        r0 = FIRST + i * HALO
        rows, dst = pl.ds(r0, HALO), pl.ds(i * HALO, HALO)
        surf = [sx[t, rows, :] for t in range(3)]
        n_val, s_val = to_north(surf, lanes8), to_south(surf, lanes8)
        for t in range(2):
            lanes = pl.ds(t * LANES, LANES)
            wet = jnp.where(own[2, t, dst, :] > 0.0, 0.25, 0.0)
            diff = sx[t, pl.ds(r0 + 1, HALO), :] - sx[t, pl.ds(r0 - 1, HALO), :]
            stage[0, dst, lanes] = surf[t]
            stage[1, dst, lanes] = own[0, t, dst, :] - wet * diff
            stage[2, dst, lanes] = own[1, t, dst, :] - wet * (n_val[t] - s_val[t])
    ends = []
    for i, ref in enumerate((surf_out, tx_out, ty_out)):
        ends.append(pltpu.make_async_copy(stage.at[i], ref, out_sem.at[i]))
    for c in ends:
        c.start()
    for c in copies + ends:
        c.wait()
    for i in range(STEP_CHUNKS, NCHUNKS):
        late_copy(i).wait()


def in_hbm(value):
    return pltpu.with_memory_space_constraint(value, pltpu.HBM)


def local(tracer, zonal, merid, surface, flow_x, flow_y, land_mask, levels):
    hbm = pl.BlockSpec(memory_space=pltpu.HBM)
    vmem = pl.BlockSpec(memory_space=pltpu.VMEM)
    wide = pltpu.VMEM((3, EXT, LANES), F32)
    n_remote = 28 + 15 + 7
    planes = 2 * LEVELS
    left = ROWS - STEP_CHUNKS * CHUNK
    args = (tracer, zonal, merid, surface, flow_x, flow_y, land_mask, levels)
    kept = pl.pallas_call(
        step_kernel,
        out_shape=(
            pltpu.VMEM((2, LEVELS, STEP_CHUNKS * CHUNK, COLS), F32),
            pltpu.VMEM((3, 3, EXT, LANES), F32),
            pltpu.VMEM((3, 2, ROWS, LANES), F32),
            pltpu.VMEM((HALO, LANES), F32),
            pltpu.VMEM((2, LEVELS, ROWS, COLS), F32),
            pltpu.VMEM((LEVELS, ROWS, COLS), jnp.bfloat16),
            pltpu.VMEM((LEVELS, ROWS, COLS), jnp.bfloat16),
            pltpu.VMEM((planes, 2, ROWS + 2 * HALO, LANES), F32),
            pltpu.VMEM((2, 2, ROWS, LANES), I32),
            pltpu.VMEM((2 * LANES, LANES), F32),
        ),
        in_specs=[hbm] * 8,
        out_specs=(vmem,) * 10,
        scratch_shapes=[
            pltpu.VMEM((2, ROWS, LANES), I32),
            pltpu.VMEM((2, ROWS, LANES), I32),
            pltpu.VMEM((2, 2, ROWS, LANES), F32),
            wide,
            pltpu.VMEM((4, 3, EXT, LANES), F32),
            wide, wide, wide, wide, wide, wide, wide, wide, wide,
            pltpu.VMEM((2 * planes, LANES), F32),
            pltpu.VMEM((2 * planes, LANES), F32),
            pltpu.VMEM((2 * planes, LANES), F32),
            pltpu.VMEM((2 * planes, LANES), F32),
            pltpu.VMEM((2 * LANES, LANES), F32),
            pltpu.VMEM((2, LANES, LANES), F32),
            pltpu.VMEM((2, planes, LANES), F32),
            pltpu.VMEM((2, planes, LANES), F32),
            pltpu.VMEM((2, planes, LANES), F32),
            pltpu.VMEM((2, planes, LANES), F32),
            pltpu.VMEM((HALO, ROWS), F32),
            pltpu.VMEM((HALO, ROWS), F32),
            pltpu.VMEM((LANES, ROWS), F32),
            pltpu.VMEM((4, HALO, LANES), F32),
            pltpu.VMEM((4, HALO, ROWS), F32),
            pltpu.VMEM((4, HALO, ROWS), F32),
            pltpu.VMEM((4, LANES, ROWS), F32),
            pltpu.VMEM((4, 4, HALO, LANES), F32),
            pltpu.VMEM((HALO, LANES), F32),
            pltpu.VMEM((HALO, LANES), F32),
            pltpu.VMEM((15, HALO, LANES), F32),
            pltpu.VMEM((7, HALO, LANES), F32),
            pltpu.SemaphoreType.DMA((10,)),
            pltpu.SemaphoreType.DMA((NGROUPS,)),
            pltpu.SemaphoreType.DMA((2,)),
            pltpu.SemaphoreType.DMA((n_remote,)),
            pltpu.SemaphoreType.DMA((n_remote,)),
        ],
        compiler_params=pltpu.CompilerParams(
            collective_id=1, has_side_effects=True, vmem_limit_bytes=20 << 20
        ),
        name="ocean_step",
    )(*[in_hbm(a) for a in args])
    return pl.pallas_call(
        finish_kernel,
        out_shape=(
            jax.ShapeDtypeStruct((2, LEVELS, ROWS, COLS), F32),
            jax.ShapeDtypeStruct((ROWS, COLS), F32),
            jax.ShapeDtypeStruct((ROWS, COLS), F32),
            jax.ShapeDtypeStruct((ROWS, COLS), F32),
        ),
        in_specs=[vmem] * 10,
        out_specs=(hbm,) * 4,
        scratch_shapes=[
            wide,
            pltpu.VMEM((3, ROWS, COLS), F32),
            pltpu.VMEM((2, LEVELS, left, COLS), F32),
            pltpu.SemaphoreType.DMA((8,)),
            pltpu.SemaphoreType.DMA((left // CHUNK,)),
            pltpu.SemaphoreType.DMA((3,)),
        ],
        compiler_params=pltpu.CompilerParams(vmem_limit_bytes=20 << 20),
        name="ocean_finish",
    )(*kept)


def solution(mesh):
    flat = P("gx", "gy")
    deep = P(None, "gx", "gy")
    full = P(None, None, "gx", "gy")
    return jax.shard_map(
        local,
        mesh=mesh,
        in_specs=(full, deep, deep, flat, flat, flat, flat, flat),
        out_specs=(full, flat, flat, flat),
        check_vma=False,
    )
```
